256 devices in a mesh: dom: 64 (over x, z, core), sub: 4 (over y).
Axes of the slice: x: 4, y: 4, z: 8, core: 2. Of those that a mesh axis runs over, the one named last changes fastest.
Arguments:
- elastic: bfloat16 [9, 35, 262144], P(None, None, ('dom', 'sub')), may hold values from -6 to 6
- jacobian: float32 [3, 262144], P(None, ('dom', 'sub')), may hold values from 0.5 to 2
- star_mats: float32 [3, 9, 9], replicated, may hold values from -2 to 2
- stiffness: bfloat16 [3, 35, 35], replicated, may hold values from -1 to 1
- face_proj: bfloat16 [4, 15, 35], replicated, may hold values from -1 to 1
- face_lift: bfloat16 [4, 35, 15], replicated, may hold values from -1.5 to 1.5
- clusters: int32 [262144], P(('dom', 'sub')), may hold values from 0 to 2
- neighbours: int32 [4, 262144], P(None, ('dom', 'sub')), may hold values from 0 to 4607, as said below
- send_faces: int32 [2, 65536], P(None, ('dom', 'sub')), may hold values from 0 to 4095, as said below
- fault_faces: int32 [32768], P(('dom', 'sub')), may hold values from 0 to 4095, as said below
- fault_strength: float32 [32768], P(('dom', 'sub')), may hold values from 0.2 to 2
- seafloor_faces: int32 [131072], P(('dom', 'sub')), may hold values from 0 to 4095, as said below
- seafloor_slots: int32 [131072], P(('dom', 'sub')), may hold values from 0 to 1023, as said below
- arrival_cells: int32 [262144], P(('dom', 'sub')), may hold values from 0 to 256, as said below
- ocean_state: float32 [3, 15, 16384], P(None, None, 'dom'), may hold values from -6 to 6
- ocean_kernels: float32 [2, 15, 15], replicated, may hold values from -1.5 to 1.5
- shallow_mats: float32 [2, 3, 3], replicated, may hold values from -3.5 to 3.5
- edge_proj: float32 [3, 5, 15], replicated, may hold values from -1.5 to 1.5
- edge_lift: float32 [3, 15, 5], replicated, may hold values from -2.5 to 2.5
- ocean_send: int32 [2, 2048], P(None, 'dom'), may hold values from 0 to 767, as said below
- ocean_neighbours: int32 [3, 16384], P(None, 'dom'), may hold values from 0 to 831, as said below
Outputs:
- elastic_next: bfloat16 [9, 35, 262144], P(None, None, ('dom', 'sub'))
- ocean_next: float32 [3, 15, 16384], P(None, None, 'dom')
The draws below stay inside these ranges and needn't reach their ends.
Inputs may be any that keep to these rules, and one draw needn't show every extreme that they name: `neighbours`: slot f * 1024 + e is face f of local element e; slot 4096 + j is the j-th trace from the block before, 4352 + j the j-th from the block after; every such received slot is named exactly once in every block. `send_faces`: local face slots; row 0 is sent to the block before, row 1 to the block after; the 512 entries of one block are distinct. `fault_faces`: local face slots, distinct in one block. `seafloor_faces`: local face slots, distinct in one block. `seafloor_slots`: distinct in one block, so at most 16 faces of a block go to one ocean block; in every block some ocean block gets exactly 16. `arrival_cells`: entry s * 16 + k of element block (d, u) is the local ocean cell of ocean block d for place k from element block (s, u); it is 256 exactly where no face arrives. `ocean_send`: local edge slots; row 0 is sent to the ocean block before, row 1 to the block after; the 64 entries of one block are distinct. `ocean_neighbours`: slot g * 256 + c is edge g of local cell c; slot 768 + j is the j-th trace from the ocean block before, 800 + j the j-th from the block after; every such received slot is named exactly once in every block.
All inputs are finite; a program needn't handle non-finite values.
Results may differ from the reference program's by a relative error of at most 0.01.
Values may be sent and summed in bfloat16 or wider, within the bound.
A program may use at most 128 MiB of HBM per device.

```python
import math
import jax
import jax.numpy as jnp
from jax import lax

NV = 9
NB = 35
NF = 15
NE = 5
NO = 3
ORDER = 3
E_DEV = 1024
CAP = 16
BF = 256
OC = 256
OBF = 32
NFAULT = 128
SF_DEV = 512
ELEMS = 262144
OCELLS = 16384
N_DOM = 64
N_SUB = 4
DEVICES = 256


def per_group(key, count, draw_device):
    device_keys = jax.random.split(key, count)
    return jax.vmap(draw_device)(device_keys)


def per_device(key, draw_device):
    return per_group(key, DEVICES, draw_device)


def distinct_slots(key, salt, count):
    slot_total = 4 * E_DEV

    def draw_device(device_key):
        shuffled = jax.random.permutation(device_key, slot_total)
        return shuffled[:count].astype(jnp.int32)
    return per_device(jax.random.fold_in(key, salt), draw_device)


def draw_neighbours(key, part):
    slot_total = 4 * E_DEV

    def draw_device(device_key):
        key_first, key_second = jax.random.split(device_key)
        shuffled = jax.random.permutation(key_first, slot_total)
        local_pick = jax.random.randint(key_second, (slot_total,), 0, slot_total)
        picked = jnp.where(shuffled < 2 * BF, slot_total + shuffled, local_pick)
        return picked.reshape(4, E_DEV).astype(jnp.int32)
    blocks = per_device(jax.random.fold_in(key, 3), draw_device)
    return jnp.moveaxis(blocks, 0, 1).reshape(4, DEVICES * E_DEV)


def draw_send_faces(key, part):
    blocks = distinct_slots(key, 5, 2 * BF).reshape(DEVICES, 2, BF)
    return jnp.moveaxis(blocks, 0, 1).reshape(2, DEVICES * BF)


def draw_fault_faces(key, part):
    return distinct_slots(key, 13, NFAULT).reshape(-1)


def draw_seafloor_faces(key, part):
    return distinct_slots(key, 17, SF_DEV).reshape(-1)


def draw_ocean_neighbours(key, part):
    slot_total = 3 * OC

    def draw_group(group_key):
        key_first, key_second = jax.random.split(group_key)
        shuffled = jax.random.permutation(key_first, slot_total)
        local_pick = jax.random.randint(key_second, (slot_total,), 0, slot_total)
        picked = jnp.where(shuffled < 2 * OBF, slot_total + shuffled, local_pick)
        return picked.reshape(3, OC).astype(jnp.int32)
    blocks = per_group(jax.random.fold_in(key, 23), N_DOM, draw_group)
    return jnp.moveaxis(blocks, 0, 1).reshape(3, N_DOM * OC)


def draw_ocean_send(key, part):
    slot_total = 3 * OC

    def draw_group(group_key):
        shuffled = jax.random.permutation(group_key, slot_total)
        return shuffled[:2 * OBF].astype(jnp.int32).reshape(2, OBF)
    blocks = per_group(jax.random.fold_in(key, 29), N_DOM, draw_group)
    return jnp.moveaxis(blocks, 0, 1).reshape(2, N_DOM * OBF)


def route_tables(key):
    base_key = jax.random.fold_in(key, 7)
    slot_count = N_DOM * CAP

    def draw_device(device_key):
        key_first, key_second = jax.random.split(device_key)
        scores = jax.random.permutation(key_first, slot_count).astype(jnp.int32)
        favoured = jax.random.randint(key_second, (), 0, N_DOM)
        positions = jnp.arange(slot_count, dtype=jnp.int32)
        scores = jnp.where(positions // CAP == favoured, -1 - positions, scores)
        ranked = jnp.argsort(scores, stable=True)
        return ranked[:SF_DEV].astype(jnp.int32)
    slot_ids = per_device(base_key, draw_device)
    chosen = jnp.zeros((DEVICES, slot_count), jnp.int32).at[jnp.arange(DEVICES)[:, None], slot_ids].set(1)
    filled = jnp.transpose(chosen.reshape(N_DOM, N_SUB, N_DOM, CAP), (2, 1, 0, 3)).reshape(DEVICES, slot_count)
    target_cells = jax.random.randint(jax.random.fold_in(base_key, 11), (DEVICES, slot_count), 0, OC)
    arrived = jnp.where(filled == 1, target_cells, OC).astype(jnp.int32)
    return (slot_ids, arrived)


def draw_seafloor_slots(key, part):
    slot_ids, arrived = route_tables(key)
    return slot_ids.reshape(-1)


def draw_arrival_cells(key, part):
    slot_ids, arrived = route_tables(key)
    return arrived.reshape(-1)


def touch_ends(entries, rng, least, top_value):
    longest = entries.shape.index(max(entries.shape))
    spots = []
    for shift in (0, 1):
        where = [jax.random.randint(jax.random.fold_in(rng, axis), (), 0, length) for axis, length in enumerate(entries.shape)]
        where[longest] = (where[longest] + shift) % entries.shape[longest]
        spots.append(tuple(where))
    return entries.at[spots[0]].set(least).at[spots[1]].set(top_value)


def shard_levels(rng, extent, pieces, least, largest):
    level = 1.0
    for dim, blocks in pieces:
        heights = jax.random.uniform(jax.random.fold_in(jax.random.fold_in(rng, 6), dim), (blocks,), jnp.float32, least / len(pieces), largest / len(pieces))
        level = level * jnp.repeat(jnp.exp(heights), extent[dim] // blocks).reshape((-1,) + (1,) * (len(extent) - 1 - dim))
    return level


def scatter_about(key, extent, spread, limit, pieces=(), held_as=jnp.bfloat16):
    values = spread * jax.random.normal(key, extent, jnp.float32)
    if pieces:
        values = values * shard_levels(key, extent, pieces, -0.22, 0.18)
    return jnp.clip(values, -limit, limit).astype(held_as)


def setup_inputs(seed: int = 0) -> dict:
    key_list = jax.random.split(jax.random.key(seed), 22)
    return {
        "elastic": scatter_about(key_list[0], (NV, NB, ELEMS), 1.0, 6.0, ((2, 256),)),
        "jacobian": jnp.clip(jnp.exp(math.log(2.0) - 1.3862944 * jax.random.uniform(key_list[1], (3, ELEMS), jnp.float32) ** shard_levels(key_list[1], (3, ELEMS), ((1, 256),), -0.2, 0.2)), 0.5, 2.0),
        "star_mats": scatter_about(key_list[2], (3, NV, NV), NV ** -0.5, 2.0, (), jnp.float32),
        "stiffness": scatter_about(key_list[3], (3, NB, NB), NB ** -0.5, 1.0),
        "face_proj": scatter_about(key_list[4], (4, NF, NB), NB ** -0.5, 1.0),
        "face_lift": scatter_about(key_list[5], (4, NB, NF), NF ** -0.5, 1.5),
        "clusters": touch_ends(jax.random.randint(key_list[6], (ELEMS,), 0, 3), jax.random.fold_in(key_list[6], 1), 0, 2).astype(jnp.int32),
        "neighbours": draw_neighbours(jax.random.fold_in(key_list[21], 71), 0),
        "send_faces": draw_send_faces(jax.random.fold_in(key_list[21], 71), 0),
        "fault_faces": draw_fault_faces(jax.random.fold_in(key_list[21], 71), 0),
        "fault_strength": jnp.clip(jnp.exp(math.log(2.0) - 2.3025851 * jax.random.uniform(key_list[10], (NFAULT * DEVICES,), jnp.float32) ** shard_levels(key_list[10], (NFAULT * DEVICES,), ((0, 256),), -0.2, 0.2)), 0.2, 2.0),
        "seafloor_faces": draw_seafloor_faces(jax.random.fold_in(key_list[21], 71), 0),
        "seafloor_slots": draw_seafloor_slots(jax.random.fold_in(key_list[21], 71), 0),
        "arrival_cells": draw_arrival_cells(jax.random.fold_in(key_list[21], 71), 0),
        "ocean_state": scatter_about(key_list[14], (NO, NF, OCELLS), 1.0, 6.0, ((2, 64),), jnp.float32),
        "ocean_kernels": scatter_about(key_list[15], (2, NF, NF), NF ** -0.5, 1.5, (), jnp.float32),
        "shallow_mats": scatter_about(key_list[16], (2, NO, NO), NO ** -0.5, 3.5, (), jnp.float32),
        "edge_proj": scatter_about(key_list[17], (3, NE, NF), NF ** -0.5, 1.5, (), jnp.float32),
        "edge_lift": scatter_about(key_list[18], (3, NF, NE), NE ** -0.5, 2.5, (), jnp.float32),
        "ocean_send": draw_ocean_send(jax.random.fold_in(key_list[21], 71), 0),
        "ocean_neighbours": draw_ocean_neighbours(jax.random.fold_in(key_list[21], 71), 0),
    }


TET_NORMALS = [[0.0, 0.0, -1.0], [0.0, -1.0, 0.0], [-1.0, 0.0, 0.0], [0.57735027, 0.57735027, 0.57735027]]
TRI_NORMALS = [[0.0, -1.0], [-1.0, 0.0], [0.70710678, 0.70710678]]
TIME_STEP = 0.5
OCEAN_STEP = 0.5
PENALTY = 1.0
HIGHEST_PREC = lax.Precision.HIGHEST


def derivative(values, jacobian, star_mats, stiffness):
    summed = jnp.zeros(values.shape, jnp.float32)
    for direction in range(3):
        moved_vals = jnp.einsum('bc,uce->ube', stiffness[direction].astype(jnp.float32), values.astype(jnp.float32))
        mixed_vals = jnp.einsum('vu,ube->vbe', star_mats[direction], moved_vals, precision=HIGHEST_PREC)
        summed = summed + jacobian[direction][None, None, :] * mixed_vals
    return summed


def predictor(elastic, jacobian, star_mats, stiffness, clusters):
    step_size = TIME_STEP * jnp.exp2(-clusters.astype(jnp.float32))
    factor = step_size
    term_bf = elastic
    integral = factor[None, None, :] * elastic.astype(jnp.float32)
    for order_idx in range(1, ORDER):
        term_bf = derivative(term_bf, jacobian, star_mats, stiffness).astype(jnp.bfloat16)
        factor = factor * step_size / (order_idx + 1)
        integral = integral + factor[None, None, :] * term_bf.astype(jnp.float32)
    return integral.astype(jnp.bfloat16)


def face_traces(integral, face_proj):
    traced = jnp.einsum('fjc,vce->vjfe', face_proj.astype(jnp.float32), integral.astype(jnp.float32)).astype(jnp.bfloat16)
    return traced.reshape(traced.shape[0], traced.shape[1], -1)


def elastic_update(elastic, integral, traced, extended, neighbours, fault_faces, fault_strength, jacobian, star_mats, stiffness, face_lift):
    own_traces = traced.astype(jnp.float32)
    beside = jnp.take(extended, neighbours, axis=2).astype(jnp.float32)
    jump_vals = beside - own_traces
    strength = jnp.zeros((own_traces.shape[2],), jnp.float32).at[fault_faces].set(fault_strength)
    safe_strength = jnp.where(strength > 0.0, strength, 1.0)
    jump_vals = jnp.where(strength > 0.0, strength * jnp.tanh(jump_vals / safe_strength), jump_vals)
    elem_count = elastic.shape[2]
    normals = jnp.array(TET_NORMALS, jnp.float32)
    normal_mats = jnp.einsum('fd,dvu->fvu', normals, star_mats, precision=HIGHEST_PREC)
    average = (own_traces + 0.5 * jump_vals).reshape(own_traces.shape[0], own_traces.shape[1], 4, elem_count)
    jump_faces = jump_vals.reshape(own_traces.shape[0], own_traces.shape[1], 4, elem_count)
    fluxes = jnp.einsum('fvu,ujfe->vjfe', normal_mats, average, precision=HIGHEST_PREC) - 0.5 * PENALTY * jump_faces
    fluxes = fluxes.astype(jnp.bfloat16)
    surface = jnp.einsum('fbj,vjfe->vbe', face_lift.astype(jnp.float32), fluxes.astype(jnp.float32))
    volume = derivative(integral, jacobian, star_mats, stiffness)
    return (elastic.astype(jnp.float32) + volume - surface).astype(jnp.bfloat16)


def ocean_edges(ocean_state, edge_proj):
    edge_vals = jnp.einsum('gkc,vce->vkge', edge_proj, ocean_state, precision=HIGHEST_PREC)
    return edge_vals.reshape(edge_vals.shape[0], edge_vals.shape[1], -1)


def ocean_update(ocean_state, source, ocean_kernels, shallow_mats, edge_proj, edge_lift, extended, ocean_neighbours):
    volume = jnp.zeros(ocean_state.shape, jnp.float32)
    for direction in range(2):
        moved_vals = jnp.einsum('bc,uce->ube', ocean_kernels[direction], ocean_state, precision=HIGHEST_PREC)
        volume = volume + jnp.einsum('vu,ube->vbe', shallow_mats[direction], moved_vals, precision=HIGHEST_PREC)
    cell_count = ocean_state.shape[2]
    edge_flat = ocean_edges(ocean_state, edge_proj)
    beside = jnp.take(extended, ocean_neighbours, axis=2)
    jump_vals = beside - edge_flat
    normal_mats = jnp.einsum('gd,dvu->gvu', jnp.array(TRI_NORMALS, jnp.float32), shallow_mats, precision=HIGHEST_PREC)
    average = (edge_flat + 0.5 * jump_vals).reshape(edge_flat.shape[0], edge_flat.shape[1], 3, cell_count)
    jump_edges = jump_vals.reshape(edge_flat.shape[0], edge_flat.shape[1], 3, cell_count)
    fluxes = jnp.einsum('gvu,ukge->vkge', normal_mats, average, precision=HIGHEST_PREC) - 0.5 * PENALTY * jump_edges
    surface = jnp.einsum('gbk,vkge->vbe', edge_lift, fluxes, precision=HIGHEST_PREC)
    updated = ocean_state + OCEAN_STEP * (volume - surface)
    return updated.at[0].add(source)


def split_count(array, count):
    shaped = array.reshape(array.shape[:-1] + (count, -1))
    return jnp.moveaxis(shaped, -2, 0)


def split_blocks(array):
    return split_count(array, DEVICES)


def reference(elastic, jacobian, star_mats, stiffness, face_proj, face_lift, clusters, neighbours, send_faces, fault_faces, fault_strength, seafloor_faces, seafloor_slots, arrival_cells, ocean_state, ocean_kernels, shallow_mats, edge_proj, edge_lift, ocean_send, ocean_neighbours):
    elem_blocks = split_blocks(elastic)
    jac_blocks = split_blocks(jacobian)
    cluster_blocks = split_blocks(clusters)
    nbr_blocks = split_blocks(neighbours).reshape(DEVICES, -1)
    send_blocks = split_blocks(send_faces)
    fault_blocks = split_blocks(fault_faces)
    strength_blocks = split_blocks(fault_strength)
    floor_blocks = split_blocks(seafloor_faces)

    def outgoing(inputs):
        elem_block, jac_blk, cluster_blk, send_blk, floor_blk = inputs
        integral = predictor(elem_block, jac_blk, star_mats, stiffness, cluster_blk)
        traced = face_traces(integral, face_proj)
        buffers = jnp.stack([jnp.take(traced, send_blk[0], axis=2), jnp.take(traced, send_blk[1], axis=2)], axis=0)
        uplift_rates = jnp.take(traced[8], floor_blk, axis=1)
        return buffers, uplift_rates

    buffers, uplift_rates = lax.map(outgoing, (elem_blocks, jac_blocks, cluster_blocks, send_blocks, floor_blocks))
    blank_block = jnp.zeros_like(buffers[:1, 0])
    from_lower = jnp.concatenate([blank_block, buffers[:-1, 1]], axis=0)
    from_upper = jnp.concatenate([buffers[1:, 0], blank_block], axis=0)

    def advance(inputs):
        elem_block, jac_blk, cluster_blk, nbr_blk, fault_blk, strength_blk, lower_ghost, upper_ghost = inputs
        integral = predictor(elem_block, jac_blk, star_mats, stiffness, cluster_blk)
        traced = face_traces(integral, face_proj)
        extended = jnp.concatenate([traced, lower_ghost, upper_ghost], axis=2)
        return elastic_update(elem_block, integral, traced, extended, nbr_blk, fault_blk, strength_blk, jac_blk, star_mats, stiffness, face_lift)

    updated = lax.map(advance, (elem_blocks, jac_blocks, cluster_blocks, nbr_blocks, fault_blocks, strength_blocks, from_lower, from_upper))
    elastic_next = jnp.moveaxis(updated, 0, -2).reshape(elastic.shape)

    slot_count = N_DOM * CAP
    slot_ids = seafloor_slots.reshape(DEVICES, SF_DEV)
    sender = jnp.arange(DEVICES, dtype=jnp.int32)[:, None]
    receiver_dom = slot_ids // CAP
    receiver = receiver_dom * N_SUB + sender % N_SUB
    position = (sender // N_SUB) * CAP + slot_ids % CAP
    arrival_table = arrival_cells.reshape(DEVICES, slot_count)
    target_cells = arrival_table[receiver, position]
    global_ids = jnp.where(target_cells < OC, receiver_dom * OC + target_cells, N_DOM * OC).astype(jnp.int32)
    values = jnp.moveaxis(uplift_rates, 1, 2).reshape(-1, NF).astype(jnp.float32)
    source = jax.ops.segment_sum(values, global_ids.reshape(-1), num_segments=N_DOM * OC + 1)[:N_DOM * OC].T

    ocean_blocks = split_count(ocean_state, N_DOM)
    source_blocks = split_count(source, N_DOM)
    onbr_blocks = split_count(ocean_neighbours, N_DOM).reshape(N_DOM, -1)
    osend_blocks = split_count(ocean_send, N_DOM)
    edge_blocks = jax.vmap(lambda state_blk: ocean_edges(state_blk, edge_proj))(ocean_blocks)
    edge_buffers = jax.vmap(lambda edges, sends: jnp.stack([jnp.take(edges, sends[0], axis=2), jnp.take(edges, sends[1], axis=2)], axis=0))(edge_blocks, osend_blocks)
    blank_edges = jnp.zeros_like(edge_buffers[:1, 0])
    ocean_from_lower = jnp.concatenate([blank_edges, edge_buffers[:-1, 1]], axis=0)
    ocean_from_upper = jnp.concatenate([edge_buffers[1:, 0], blank_edges], axis=0)
    extended_edges = jnp.concatenate([edge_blocks, ocean_from_lower, ocean_from_upper], axis=3)

    def ocean_block(state_blk, source_blk, ext_blk, onbr_blk):
        return ocean_update(state_blk, source_blk, ocean_kernels, shallow_mats, edge_proj, edge_lift, ext_blk, onbr_blk)

    ocean_new = jax.vmap(ocean_block)(ocean_blocks, source_blocks, extended_edges, onbr_blocks)
    ocean_next = jnp.moveaxis(ocean_new, 0, -2).reshape(ocean_state.shape)
    return elastic_next, ocean_next
```

```python
import functools

import jax
import jax.numpy as jnp
from jax import lax
from jax.experimental import pallas as pl
from jax.experimental.pallas import tpu as pltpu
from jax.sharding import PartitionSpec as P

MESH = pl.DeviceIdType.MESH
F32, BF16 = jnp.float32, jnp.bfloat16
HIGHEST = lax.Precision.HIGHEST

NV, NB, NF = 9, 35, 15
NO, NE = 3, 5
ROWS = 320
E = 1024
BF = 256
OC, OBF = 256, 32
CAP = 16
N_DOM, N_SUB = 64, 4
CHUNK = 256
ROOT3 = 0.57735027
ROOT2 = 0.70710678
TET = [
    [(2, -1.0)],
    [(1, -1.0)],
    [(0, -1.0)],
    [(0, ROOT3), (1, ROOT3), (2, ROOT3)],
]
TRI = [[(1, -1.0)], [(0, -1.0)], [(0, ROOT2), (1, ROOT2)]]


def iota(shape, dim):
    return lax.broadcasted_iota(jnp.int32, shape, dim)


def div35(x):
    return lax.shift_right_logical(x * 1873, 16)


def div15(x):
    return lax.shift_right_logical(x * 4370, 16)


def div5(x):
    return lax.shift_right_logical(x * 13108, 16)


def onehot(cond, dtype=BF16):
    return jnp.where(cond, 1.0, 0.0).astype(dtype)


def dot(a, b, precision=None):
    return lax.dot_general(
        a, b, (((1,), (0,)), ((), ())), precision=precision, preferred_element_type=F32
    )


def dot_tn(a, b, precision=None):
    return lax.dot_general(
        a, b, (((0,), (0,)), ((), ())), precision=precision, preferred_element_type=F32
    )


def dot_nt(a, b, precision=None):
    return lax.dot_general(
        a, b, (((1,), (1,)), ((), ())), precision=precision, preferred_element_type=F32
    )


def split(x):
    high = x.astype(BF16)
    return high, (x - high.astype(F32)).astype(BF16)


def combine(mats, pairs):
    total = None
    for direction, factor in pairs:
        term = mats[direction] * factor
        total = term if total is None else total + term
    return total


def spread(select_rows, mat, select_cols):
    high, low = split(mat)
    high = dot(high, select_cols).astype(BF16)
    low = dot(low, select_cols).astype(BF16)
    return dot(select_rows, high) + dot(select_rows, low)


def kernel(
    elastic,
    jac,
    star,
    stiff,
    fproj,
    flift,
    clusters,
    nbr_s,
    send_s,
    fault,
    strength,
    floor_s,
    slots,
    arrival,
    ocean,
    okern,
    shal,
    eproj,
    elift,
    osend_s,
    onbr_s,
    out_e,
    out_o,
    xf,
    xs,
    wmat,
    fmat,
    mmat,
    ext,
    beside,
    jm,
    accf,
    stage,
    fsend,
    frecv,
    oext,
    obeside,
    osend,
    orecv,
    ost,
    oacc,
    upl,
    pack,
    asend,
    arecv,
    part,
    fsend_sem,
    frecv_sem,
    osend_sem,
    orecv_sem,
    asend_sem,
    arecv_sem,
    psend_sem,
    precv_sem,
):
    dom = lax.axis_index("dom")
    sub = lax.axis_index("sub")
    block = dom * N_SUB + sub
    n_blocks = N_DOM * N_SUB
    after = lax.rem(block + 1, n_blocks)
    before = lax.rem(block + n_blocks - 1, n_blocks)
    after_id = (lax.div(after, N_SUB), lax.rem(after, N_SUB))
    before_id = (lax.div(before, N_SUB), lax.rem(before, N_SUB))
    dom_after = lax.rem(dom + 1, N_DOM)
    dom_before = lax.rem(dom + N_DOM - 1, N_DOM)

    barrier = pltpu.get_barrier_semaphore()

    def greet(k, carry):
        there = (lax.rem(dom + k, N_DOM), sub)
        pl.semaphore_signal(barrier, inc=1, device_id=there, device_id_type=MESH)
        return carry

    lax.fori_loop(1, N_DOM, greet, 0)
    for k in range(1, N_SUB):
        there = (dom, lax.rem(sub + k, N_SUB))
        pl.semaphore_signal(barrier, inc=1, device_id=there, device_id_type=MESH)
    for there in (before_id, after_id):
        pl.semaphore_signal(barrier, inc=1, device_id=there, device_id_type=MESH)

    row = iota((ROWS, 1), 0)
    row_v = div35(row)
    row_b = row - NB * row_v
    pick_v = onehot(row_v == iota((ROWS, NV), 1))
    pick_b = onehot(row_b == iota((ROWS, NB), 1))

    col = iota((1, 3 * ROWS), 1)
    col_d = (col >= ROWS).astype(jnp.int32) + (col >= 2 * ROWS).astype(jnp.int32)
    col_r = col - ROWS * col_d
    col_u = div35(col_r)
    col_c = col_r - NB * col_u
    a_high, a_low, k_cols = None, None, None
    for d in range(3):
        sel_u = onehot((col_d == d) & (col_u == iota((NV, 3 * ROWS), 0)))
        sel_c = onehot((col_d == d) & (col_c == iota((NB, 3 * ROWS), 0)))
        high, low = split(star[d])
        terms = (dot(high, sel_u), dot(low, sel_u), dot(stiff[d], sel_c))
        if d == 0:
            a_high, a_low, k_cols = terms
        else:
            a_high, a_low, k_cols = (
                a_high + terms[0],
                a_low + terms[1],
                k_cols + terms[2],
            )
    a_high, a_low, k_cols = a_high.astype(BF16), a_low.astype(BF16), k_cols.astype(BF16)
    wmat[:, : 3 * ROWS] = (
        (dot(pick_v, a_high) + dot(pick_v, a_low)) * dot(pick_b, k_cols)
    ).astype(BF16)

    q = iota((1, 256), 1)
    q_g = div15(q)
    q_u = jnp.where(q_g == 0, NV - 1, q_g - 1)
    q_j = q - NF * q_g
    q_ok = q_g < NV
    sel_j = onehot((q_j == iota((NF, 256), 0)) & q_ok)
    same_var = (row_v == q_u) & q_ok
    for f in range(4):
        proj = dot_tn(fproj[f], sel_j).astype(BF16)
        fmat[:, f * 256 : (f + 1) * 256] = jnp.where(
            same_var, dot(pick_b, proj), 0.0
        ).astype(BF16)

    for v in range(NV):
        xf[NB * v : NB * (v + 1), :] = elastic[v].astype(F32)
    xf[NV * NB :, :] = jnp.zeros((ROWS - NV * NB, E), F32)

    step = 0.5 * jnp.exp2(-clusters[...].astype(F32))
    for c in range(E // CHUNK):
        cols = slice(c * CHUNK, (c + 1) * CHUNK)

        def scaled(x):
            for d in range(3):
                xs[d * ROWS : (d + 1) * ROWS, cols] = (jac[d : d + 1, cols] * x).astype(
                    BF16
                )

        h = step[:, cols]
        x = xf[:, cols]
        scaled(x)
        term = dot(wmat[:, : 3 * ROWS], xs[: 3 * ROWS, cols])
        integral = h * x + (h * h * 0.5) * term
        scaled(term)
        term = dot(wmat[:, : 3 * ROWS], xs[: 3 * ROWS, cols])
        integral = (integral + (h * h * h * (1.0 / 6.0)) * term).astype(BF16)
        xs[3 * ROWS :, cols] = integral
        scaled(integral.astype(F32))
        traced = dot_tn(integral, fmat[...])
        for f in range(4):
            for half in range(2):
                lanes = slice((2 * f + half) * 128, (2 * f + half + 1) * 128)
                ext[half, f * E + c * CHUNK : f * E + (c + 1) * CHUNK, :] = traced[:, lanes]

    def gather_send(i, carry):
        for k in range(8):
            j = i * 8 + k
            for side in range(2):
                slot = send_s[side, j]
                for half in range(2):
                    stage[side, half, pl.ds(j, 1), :] = ext[half, pl.ds(slot, 1), :]
            for part_ in range(2):
                m = part_ * 256 + j
                upl[pl.ds(m, 1), :] = ext[0, pl.ds(floor_s[m], 1), :]
        return carry

    lax.fori_loop(0, BF // 8, gather_send, 0)
    fsend[...] = stage[...].astype(BF16)

    pl.semaphore_wait(barrier, N_DOM - 1 + N_SUB - 1 + 2)
    face_copies = []
    for side, there in ((0, before_id), (1, after_id)):
        copy = pltpu.make_async_remote_copy(
            src_ref=fsend.at[side],
            dst_ref=frecv.at[1 - side],
            send_sem=fsend_sem.at[side],
            recv_sem=frecv_sem.at[1 - side],
            device_id=there,
            device_id_type=MESH,
        )
        copy.start()
        face_copies.append(copy)

    lane = iota((1, 128), 1)
    moved = jnp.where(lane < NF, upl[...], 0.0)
    for shift in (16, 32, 64):
        moved = moved + pltpu.roll(moved, shift, 1)
    moved = moved.astype(BF16)
    places = iota((128, 1), 0) * 8
    packed = jnp.zeros((128, 128), F32)
    for p in range(8):
        hits = onehot(slots[...] == places + p)
        packed = packed + jnp.where(
            lax.shift_right_logical(lane, 4) == p, dot(hits, moved), 0.0
        )
    pack[...] = packed
    for d in range(N_DOM):
        asend[d] = pack[2 * d : 2 * d + 2, :]
    arecv[dom] = asend[dom]

    def send_floor(k, carry):
        there = lax.rem(dom + k, N_DOM)
        pltpu.make_async_remote_copy(
            src_ref=asend.at[there],
            dst_ref=arecv.at[dom],
            send_sem=asend_sem,
            recv_sem=arecv_sem,
            device_id=(there, sub),
            device_id_type=MESH,
        ).start()
        return carry

    lax.fori_loop(1, N_DOM, send_floor, 0)

    orow = iota((48, 1), 0)
    orow_v = div15(orow)
    orow_b = orow - NF * orow_v
    opick_v = onehot(orow_v == iota((48, NO), 1), F32)
    opick_b = onehot(orow_b == iota((48, NF), 1), F32)
    o_u = div5(lane)
    o_k = lane - NE * o_u
    o_ok = o_u < NO
    osel_k = onehot((o_k == iota((NE, 128), 0)) & o_ok, F32)
    osel_u = onehot((o_u == iota((NO, 128), 0)) & o_ok, F32)
    for v in range(NO):
        ost[NF * v : NF * (v + 1), :] = ocean[v]
    ost[NO * NF :, :] = jnp.zeros((48 - NO * NF, OC), F32)
    for g in range(3):
        proj = dot(opick_b, dot_tn(eproj[g], osel_k, HIGHEST), HIGHEST)
        proj = jnp.where((orow_v == o_u) & o_ok, proj, 0.0)
        oext[g * OC : (g + 1) * OC, :] = dot_tn(ost[...], proj, HIGHEST)
    for side in range(2):
        for j in range(OBF):
            osend[side, j : j + 1, :] = oext[pl.ds(osend_s[side, j], 1), :]
    ocean_copies = []
    for side, there in ((0, (dom_before, sub)), (1, (dom_after, sub))):
        copy = pltpu.make_async_remote_copy(
            src_ref=osend.at[side],
            dst_ref=orecv.at[1 - side],
            send_sem=osend_sem.at[side],
            recv_sem=orecv_sem.at[1 - side],
            device_id=there,
            device_id_type=MESH,
        )
        copy.start()
        ocean_copies.append(copy)

    stars = [star[d] for d in range(3)]
    eye = onehot(iota((NV, NV), 0) == iota((NV, NV), 1), F32)
    sel_u = onehot((q_u == iota((NV, 256), 0)) & q_ok)
    own = [None, None, None]
    for f in range(4):
        normal = 0.5 * (eye - combine(stars, TET[f]))
        lifts = dot(pick_b, dot(flift[f], sel_j).astype(BF16))
        mmat[:, f * 256 : (f + 1) * 256] = (spread(pick_v, normal, sel_u) * lifts).astype(
            BF16
        )
        through = dot(flift[f], fproj[f])
        for d, factor in TET[f]:
            term = through * -factor
            own[d] = term if own[d] is None else own[d] + term
    last = iota((1, ROWS), 1)
    last_u = div35(last)
    last_c = last - NB * last_u
    sel_u4 = onehot(last_u == iota((NV, ROWS), 0))
    sel_c4 = onehot(last_c == iota((NB, ROWS), 0))
    total = jnp.zeros((ROWS, ROWS), F32)
    for d in range(3):
        total = total + spread(pick_v, stars[d], sel_u4) * spread(pick_b, own[d], sel_c4)
    wmat[:, 3 * ROWS :] = total.astype(BF16)
    for c in range(E // CHUNK):
        cols = slice(c * CHUNK, (c + 1) * CHUNK)
        accf[:, cols] = xf[:, cols] + dot(wmat[...], xs[:, cols])

    for side in range(2):
        face_copies[side].wait_recv()
    has_before = (block > 0).astype(F32)
    has_after = (block < n_blocks - 1).astype(F32)
    ext[:, 4 * E : 4 * E + BF, :] = frecv[0].astype(F32) * has_before
    ext[:, 4 * E + BF : 4 * E + 2 * BF, :] = frecv[1].astype(F32) * has_after

    def gather(i, carry):
        for k in range(4):
            e = i * 4 + k
            for f in range(4):
                slot = nbr_s[f, e]
                for half in range(2):
                    beside[half, pl.ds(f * E + e, 1), :] = ext[half, pl.ds(slot, 1), :]
        return carry

    lax.fori_loop(0, E // 4, gather, 0)

    pltpu.make_async_copy(
        arecv.at[pl.ds(0, N_DOM - 1)], arecv.at[pl.ds(0, N_DOM - 1)], arecv_sem
    ).wait()
    for s in range(N_DOM):
        pack[2 * s : 2 * s + 2, :] = arecv[s]
    arrived = pack[...].astype(BF16)
    wide = iota((1, 1024), 1)
    wide_l = wide & 127
    wide_q = lax.shift_right_logical(wide, 7)
    pick_a = onehot(iota((128, 1), 0) == 8 * (wide_l & 15) + wide_q)
    targets = dot(arrival[...].astype(F32).astype(BF16), pick_a)
    targets = jnp.where(
        iota((8, 1), 0) == lax.shift_right_logical(wide_l, 4), targets, 0.0
    )
    targets = jnp.sum(targets, axis=0, keepdims=True)
    cells = iota((OC, 1), 0).astype(F32)
    forced = jnp.zeros((OC, 128), F32)
    for p in range(8):
        hits = onehot(targets[:, p * 128 : (p + 1) * 128] == cells)
        forced = forced + jnp.where(
            lax.shift_right_logical(lane, 4) == p, dot(hits, arrived), 0.0
        )
    fold = onehot((lane & 15) == iota((16, 128), 0), F32)
    part[sub] = dot_nt(fold, forced, HIGHEST)
    part_copies = []
    for k in range(1, N_SUB):
        copy = pltpu.make_async_remote_copy(
            src_ref=part.at[sub],
            dst_ref=part.at[sub],
            send_sem=psend_sem.at[k - 1],
            recv_sem=precv_sem.at[k - 1],
            device_id=(dom, lax.rem(sub + k, N_SUB)),
            device_id_type=MESH,
        )
        copy.start()
        part_copies.append(copy)

    rates = jnp.transpose(jnp.broadcast_to(strength[...], (128, 128)))
    rate_high, rate_low = split(rates)
    for f in range(4):
        on_fault = onehot(fault[...] == iota((E, 1), 0) + f * E)
        limit = dot(on_fault, rate_high) + dot(on_fault, rate_low)
        frictional = limit > 0.0
        inverse = 1.0 / jnp.where(frictional, limit, 1.0)
        for half in range(2):
            rows = slice(f * E, (f + 1) * E)
            jump = beside[half, rows, :] - ext[half, rows, :]
            jump = jnp.where(frictional, limit * jnp.tanh(jump * inverse), jump)
            jm[:, f * 256 + half * 128 : f * 256 + (half + 1) * 128] = jump.astype(BF16)
    for c in range(E // CHUNK):
        cols = slice(c * CHUNK, (c + 1) * CHUNK)
        accf[:, cols] = accf[:, cols] + dot_nt(mmat[...], jm[cols, :])
    for v in range(NV):
        out_e[v] = accf[NB * v : NB * (v + 1), :].astype(BF16)

    for side in range(2):
        ocean_copies[side].wait_recv()
    oext[3 * OC : 3 * OC + OBF, :] = orecv[0] * (dom > 0).astype(F32)
    oext[3 * OC + OBF :, :] = orecv[1] * (dom < N_DOM - 1).astype(F32)

    def ocean_gather(i, carry):
        for k in range(4):
            for g in range(3):
                obeside[pl.ds(g * OC + i * 4 + k, 1), :] = oext[
                    pl.ds(onbr_s[g, i * 4 + k], 1), :
                ]
        return carry

    lax.fori_loop(0, OC // 4, ocean_gather, 0)
    shals = [shal[d] for d in range(2)]
    oeye = onehot(iota((NO, NO), 0) == iota((NO, NO), 1), F32)
    inner = [okern[0], okern[1]]
    updated = ost[...]
    for g in range(3):
        through = dot(elift[g], eproj[g], HIGHEST)
        for d, factor in TRI[g]:
            inner[d] = inner[d] - factor * through
        normal = 0.25 * (oeye - combine(shals, TRI[g]))
        outer = dot(opick_v, dot(normal, osel_u, HIGHEST), HIGHEST)
        lifts = dot(opick_b, dot(elift[g], osel_k, HIGHEST), HIGHEST)
        ojump = obeside[g * OC : (g + 1) * OC, :] - oext[g * OC : (g + 1) * OC, :]
        updated = updated + dot_nt(outer * lifts, ojump, HIGHEST)
    volume = jnp.zeros((48, 48), F32)
    for d in range(2):
        left = dot_nt(dot(opick_v, shals[d], HIGHEST), opick_v, HIGHEST)
        right = dot_nt(dot(opick_b, inner[d], HIGHEST), opick_b, HIGHEST)
        volume = volume + left * right
    updated = updated + 0.5 * dot(volume, ost[...], HIGHEST)
    oacc[...] = updated
    for copy in part_copies:
        copy.wait_recv()
    source = part[0] + part[1] + part[2] + part[3]
    oacc[:16, :] = oacc[:16, :] + source
    for v in range(NO):
        out_o[v] = oacc[NF * v : NF * (v + 1), :]

    for copy in face_copies + ocean_copies + part_copies:
        copy.wait_send()
    pltpu.make_async_copy(
        asend.at[pl.ds(0, N_DOM - 1)], asend.at[pl.ds(0, N_DOM - 1)], asend_sem
    ).wait()


def body(
    elastic,
    jacobian,
    star_mats,
    stiffness,
    face_proj,
    face_lift,
    clusters,
    neighbours,
    send_faces,
    fault_faces,
    fault_strength,
    seafloor_faces,
    seafloor_slots,
    arrival_cells,
    ocean_state,
    ocean_kernels,
    shallow_mats,
    edge_proj,
    edge_lift,
    ocean_send,
    ocean_neighbours,
):
    vmem = pl.BlockSpec(memory_space=pltpu.VMEM)
    smem = pl.BlockSpec(memory_space=pltpu.SMEM)
    specs = [vmem] * 7 + [smem] * 2 + [vmem] * 2 + [smem] + [vmem] * 7 + [smem] * 2
    dma = pltpu.SemaphoreType.DMA
    return pl.pallas_call(
        kernel,
        out_shape=(
            jax.ShapeDtypeStruct(elastic.shape, BF16),
            jax.ShapeDtypeStruct(ocean_state.shape, F32),
        ),
        in_specs=specs,
        out_specs=(vmem, vmem),
        scratch_shapes=[
            pltpu.VMEM((ROWS, E), F32),
            pltpu.VMEM((4 * ROWS, E), BF16),
            pltpu.VMEM((ROWS, 4 * ROWS), BF16),
            pltpu.VMEM((ROWS, 1024), BF16),
            pltpu.VMEM((ROWS, 1024), BF16),
            pltpu.VMEM((2, 4 * E + 2 * BF, 128), F32),
            pltpu.VMEM((2, 4 * E, 128), F32),
            pltpu.VMEM((E, 1024), BF16),
            pltpu.VMEM((ROWS, E), F32),
            pltpu.VMEM((2, 2, BF, 128), F32),
            pltpu.VMEM((2, 2, BF, 128), BF16),
            pltpu.VMEM((2, 2, BF, 128), BF16),
            pltpu.VMEM((3 * OC + 2 * OBF, 128), F32),
            pltpu.VMEM((3 * OC, 128), F32),
            pltpu.VMEM((2, OBF, 128), F32),
            pltpu.VMEM((2, OBF, 128), F32),
            pltpu.VMEM((48, OC), F32),
            pltpu.VMEM((48, OC), F32),
            pltpu.VMEM((512, 128), F32),
            pltpu.VMEM((128, 128), F32),
            pltpu.VMEM((N_DOM, 2, 128), F32),
            pltpu.VMEM((N_DOM, 2, 128), F32),
            pltpu.VMEM((N_SUB, 16, OC), F32),
            dma((2,)),
            dma((2,)),
            dma((2,)),
            dma((2,)),
            dma,
            dma,
            dma((3,)),
            dma((3,)),
        ],
        compiler_params=pltpu.CompilerParams(
            collective_id=0,
            has_side_effects=True,
            vmem_limit_bytes=48 * 1024 * 1024,
        ),
    )(
        elastic,
        jacobian,
        star_mats,
        stiffness,
        face_proj,
        face_lift,
        clusters.reshape(1, E),
        neighbours,
        send_faces,
        fault_faces.reshape(1, 128),
        fault_strength.reshape(1, 128),
        seafloor_faces,
        seafloor_slots.reshape(1, 512),
        arrival_cells.reshape(8, 128),
        ocean_state,
        ocean_kernels,
        shallow_mats,
        edge_proj,
        edge_lift,
        ocean_send,
        ocean_neighbours,
    )


def solution(mesh):
    both = ("dom", "sub")
    return jax.shard_map(
        body,
        mesh=mesh,
        in_specs=(
            P(None, None, both),
            P(None, both),
            P(),
            P(),
            P(),
            P(),
            P(both),
            P(None, both),
            P(None, both),
            P(both),
            P(both),
            P(both),
            P(both),
            P(both),
            P(None, None, "dom"),
            P(),
            P(),
            P(),
            P(),
            P(None, "dom"),
            P(None, "dom"),
        ),
        out_specs=(P(None, None, both), P(None, None, "dom")),
        check_vma=False,
    )
```

```python
import functools

import jax
import jax.numpy as jnp
from jax import lax
from jax.experimental import pallas as pl
from jax.experimental.pallas import tpu as pltpu
from jax.sharding import PartitionSpec as P

MESH = pl.DeviceIdType.MESH
F32, BF16 = jnp.float32, jnp.bfloat16
HIGHEST = lax.Precision.HIGHEST

NV, NB, NF = 9, 35, 15
NO, NE = 3, 5
ROWS = 320
E = 1024
BF = 256
OC, OBF = 256, 32
CAP = 16
N_DOM, N_SUB = 64, 4
CHUNK = 256
MAIN = 128
LEAD = 8
REST = 4 * E + 2 * BF + 2 * LEAD
ROOT3 = 0.57735027
ROOT2 = 0.70710678
TET = [
    [(2, -1.0)],
    [(1, -1.0)],
    [(0, -1.0)],
    [(0, ROOT3), (1, ROOT3), (2, ROOT3)],
]
TRI = [[(1, -1.0)], [(0, -1.0)], [(0, ROOT2), (1, ROOT2)]]


def iota(shape, dim):
    return lax.broadcasted_iota(jnp.int32, shape, dim)


def div35(x):
    return lax.shift_right_logical(x * 1873, 16)


def div15(x):
    return lax.shift_right_logical(x * 4370, 16)


def div5(x):
    return lax.shift_right_logical(x * 13108, 16)


def onehot(cond, dtype=BF16):
    return jnp.where(cond, 1.0, 0.0).astype(dtype)


def dot(a, b, precision=None):
    return lax.dot_general(
        a, b, (((1,), (0,)), ((), ())), precision=precision, preferred_element_type=F32
    )


def dot_tn(a, b, precision=None):
    return lax.dot_general(
        a, b, (((0,), (0,)), ((), ())), precision=precision, preferred_element_type=F32
    )


def dot_nt(a, b, precision=None):
    return lax.dot_general(
        a, b, (((1,), (1,)), ((), ())), precision=precision, preferred_element_type=F32
    )


def split(x):
    high = x.astype(BF16)
    return high, (x - high.astype(F32)).astype(BF16)


def combine(mats, pairs):
    total = None
    for direction, factor in pairs:
        term = mats[direction] * factor
        total = term if total is None else total + term
    return total


def spread(select_rows, mat, select_cols):
    return dot(select_rows, dot(mat.astype(BF16), select_cols).astype(BF16))


def face_columns(q):
    group = div15(q)
    variable = jnp.where(group == 0, NV - 1, group - 1)
    return variable, q - NF * group, group < NV


def main_kernel(
    elastic_h,
    jac_h,
    star_h,
    stiff_h,
    fproj_h,
    flift_h,
    clusters_h,
    nbr_h,
    send_h,
    fault_h,
    strength_h,
    floor_h,
    slots_h,
    arrival_h,
    ocean_h,
    okern_h,
    shal_h,
    eproj_h,
    elift_h,
    osend_h,
    onbr_h,
    fault1_h,
    out_e_h,
    out_o_h,
    elastic,
    jac,
    star,
    stiff,
    fproj,
    flift,
    clusters,
    nbr_s,
    send_s,
    fault,
    fault_s,
    strength,
    floor_s,
    slots,
    arrival,
    ocean,
    okern,
    shal,
    eproj,
    elift,
    osend_s,
    onbr_s,
    in_sem,
    xf,
    xs,
    wmat,
    fmat,
    mmat,
    accf,
    ext,
    jm,
    fjump,
    fjump_rest,
    fsend,
    frecv,
    out_e,
    out_o,
    oacc,
    oext,
    obeside,
    osend,
    orecv,
    ost,
    upl,
    pack,
    asend,
    arecv,
    part,
    fsend_sem,
    frecv_sem,
    osend_sem,
    orecv_sem,
    asend_sem,
    arecv_sem,
    psend_sem,
    precv_sem,
    out_sem,
):
    loads = {}
    pairs = (
        ("star", star_h, star),
        ("stiff", stiff_h, stiff),
        ("elastic", elastic_h, elastic),
        ("jac", jac_h, jac),
        ("clusters", clusters_h, clusters),
        ("fproj", fproj_h, fproj),
        ("floor", floor_h, floor_s),
        ("slots", slots_h, slots),
        ("send_s", send_h, send_s),
        ("nbr_s", nbr_h, nbr_s),
        ("flift", flift_h, flift),
        ("arrival", arrival_h, arrival),
        ("fault", fault_h, fault),
        ("fault_s", fault1_h, fault_s),
        ("strength", strength_h, strength),
        ("ocean", ocean_h, ocean),
        ("eproj", eproj_h, eproj),
        ("osend", osend_h, osend_s),
        ("onbr", onbr_h, onbr_s),
        ("okern", okern_h, okern),
        ("shal", shal_h, shal),
        ("elift", elift_h, elift),
    )
    for n, (name, source, target) in enumerate(pairs):
        loads[name] = pltpu.make_async_copy(source, target, in_sem.at[n])
        loads[name].start()

    dom = lax.axis_index("dom")
    sub = lax.axis_index("sub")
    block = dom * N_SUB + sub
    n_blocks = N_DOM * N_SUB
    after = lax.rem(block + 1, n_blocks)
    before = lax.rem(block + n_blocks - 1, n_blocks)
    after_id = (lax.div(after, N_SUB), lax.rem(after, N_SUB))
    before_id = (lax.div(before, N_SUB), lax.rem(before, N_SUB))
    dom_after = lax.rem(dom + 1, N_DOM)
    dom_before = lax.rem(dom + N_DOM - 1, N_DOM)

    barrier = pltpu.get_barrier_semaphore()

    def greet(i, carry):
        for k in range(1, 10):
            there = (lax.rem(dom + i * 9 + k, N_DOM), sub)
            pl.semaphore_signal(barrier, inc=1, device_id=there, device_id_type=MESH)
        return carry

    lax.fori_loop(0, 7, greet, 0)
    for k in range(1, N_SUB):
        there = (dom, lax.rem(sub + k, N_SUB))
        pl.semaphore_signal(barrier, inc=1, device_id=there, device_id_type=MESH)
    for there in (before_id, after_id):
        pl.semaphore_signal(barrier, inc=1, device_id=there, device_id_type=MESH)

    row = iota((ROWS, 1), 0)
    row_v = div35(row)
    row_b = row - NB * row_v
    pick_v = onehot(row_v == iota((ROWS, NV), 1))
    pick_b = onehot(row_b == iota((ROWS, NB), 1))

    col = iota((1, 3 * ROWS), 1)
    col_d = (col >= ROWS).astype(jnp.int32) + (col >= 2 * ROWS).astype(jnp.int32)
    col_r = col - ROWS * col_d
    col_u = div35(col_r)
    col_c = col_r - NB * col_u
    loads["star"].wait()
    loads["stiff"].wait()
    stars = [star[:, d, :] for d in range(3)]
    a_cols, k_cols = None, None
    for d in range(3):
        sel_u = onehot((col_d == d) & (col_u == iota((NV, 3 * ROWS), 0)))
        sel_c = onehot((col_d == d) & (col_c == iota((NB, 3 * ROWS), 0)))
        terms = (dot(stars[d].astype(BF16), sel_u), dot(stiff[d], sel_c))
        if d == 0:
            a_cols, k_cols = terms
        else:
            a_cols, k_cols = a_cols + terms[0], k_cols + terms[1]
    wmat[:, : 3 * ROWS] = (
        dot(pick_v, a_cols.astype(BF16)) * dot(pick_b, k_cols.astype(BF16))
    ).astype(BF16)

    loads["elastic"].wait()
    for v in range(NV):
        xf[NB * v : NB * (v + 1), :] = elastic[v].astype(F32)
    xf[NV * NB :, :] = jnp.zeros((ROWS - NV * NB, E), F32)
    loads["jac"].wait()
    loads["clusters"].wait()
    step = 0.5 * jnp.exp2(-clusters[...].astype(F32))
    chunks = [slice(c * CHUNK, (c + 1) * CHUNK) for c in range(E // CHUNK)]

    def scaled(x, cols):
        for d in range(3):
            xs[d * ROWS : (d + 1) * ROWS, cols] = (jac[d : d + 1, cols] * x).astype(BF16)

    for cols in chunks:
        scaled(xf[:, cols], cols)

    loads["fproj"].wait()
    fprojs = fproj[...].astype(F32)
    fprojs = [fprojs[:, f, :].astype(BF16) for f in range(4)]
    lane = iota((1, 128), 1)
    q_u, q_j, q_ok = face_columns(lane)
    r_lane = lane & 31
    r_u, r_j, r_ok = face_columns(MAIN + r_lane)
    r_ok = r_ok & (r_lane < 8)
    halves = ((q_u, q_j, q_ok), (r_u, r_j, r_ok))
    sel_j = [onehot((h_j == iota((NF, MAIN), 0)) & h_ok) for h_u, h_j, h_ok in halves]
    for half, (h_u, h_j, h_ok) in enumerate(halves):
        pair_u = jnp.concatenate([jnp.where(h_ok, h_u, -1)] * 2, axis=1)
        for f in range(0, 4, 2):
            proj = [dot_tn(fprojs[f + n], sel_j[half]).astype(BF16) for n in range(2)]
            proj = dot(pick_b, jnp.concatenate(proj, axis=1))
            fmat[:, (4 * half + f) * MAIN : (4 * half + f + 2) * MAIN] = jnp.where(
                row_v == pair_u, proj, 0.0
            ).astype(BF16)

    for cols in chunks:
        h = step[:, cols]
        term = dot(wmat[:, : 3 * ROWS], xs[: 3 * ROWS, cols])
        accf[:, cols] = h * xf[:, cols] + (h * h * 0.5) * term
        scaled(term, cols)
    for cols in chunks:
        h = step[:, cols]
        term = dot(wmat[:, : 3 * ROWS], xs[: 3 * ROWS, cols])
        integral = (accf[:, cols] + (h * h * h * (1.0 / 6.0)) * term).astype(BF16)
        xs[3 * ROWS :, cols] = integral
    for c, cols in enumerate(chunks):
        traced = dot_tn(xs[3 * ROWS :, cols], fmat[...])
        for f in range(4):
            rows = slice(LEAD + f * E + c * CHUNK, LEAD + f * E + (c + 1) * CHUNK)
            ext[rows, :] = traced[:, f * MAIN : (f + 1) * MAIN]
            rows = slice(REST + rows.start, REST + rows.stop)
            ext[rows, :] = traced[:, (4 + f) * MAIN : (5 + f) * MAIN]

    sublane = iota((8, 128), 0)

    def rows8(table, slots8, start=LEAD):
        taken = table[pl.ds(slots8[0] + start, 8), :]
        for k in range(1, 8):
            taken = jnp.where(
                sublane == k, table[pl.ds(slots8[k] + (start - k), 8), :], taken
            )
        return taken

    loads["floor"].wait()
    loads["slots"].wait()
    loads["send_s"].wait()

    def gather_floor(i, carry):
        for k in range(4):
            first = pl.multiple_of(i * 32 + 8 * k, 8)
            upl[pl.ds(first, 8), :] = rows8(ext, [floor_s[first + n] for n in range(8)])
        return carry

    lax.fori_loop(0, 512 // 32, gather_floor, 0)
    moved = jnp.where(lane < NF, upl[...], 0.0)
    for shift in (16, 32, 64):
        moved = moved + pltpu.roll(moved, shift, 1)
    moved = moved.astype(BF16)
    places = iota((128, 1), 0) * 8
    packed = jnp.zeros((128, 128), F32)
    for p in range(8):
        hits = onehot(slots[...] == places + p)
        packed = packed + jnp.where(
            lax.shift_right_logical(lane, 4) == p, dot(hits, moved), 0.0
        )
    pack[...] = packed
    for d in range(N_DOM):
        asend[d] = pack[2 * d : 2 * d + 2, :]
    arecv[dom] = asend[dom]

    pl.semaphore_wait(barrier, N_DOM - 1 + N_SUB - 1 + 2)

    def send_floor(i, carry):
        for k in range(1, 10):
            there = lax.rem(dom + i * 9 + k, N_DOM)
            pltpu.make_async_remote_copy(
                src_ref=asend.at[there],
                dst_ref=arecv.at[dom],
                send_sem=asend_sem,
                recv_sem=arecv_sem,
                device_id=(there, sub),
                device_id_type=MESH,
            ).start()
        return carry

    lax.fori_loop(0, 7, send_floor, 0)

    for part_ in range(BF // 128):

        def gather_send(i, carry):
            first = pl.multiple_of(i * 16, 16)
            for side in range(2):
                slots = [send_s[part_ * 256 + side * 128 + first + n] for n in range(16)]
                for half, start in enumerate((LEAD, LEAD + REST)):
                    taken = [rows8(ext, slots[8 * h : 8 * h + 8], start) for h in range(2)]
                    rows = pl.ds(part_ * 128 + first, 16)
                    fsend[side, half, rows, :] = jnp.concatenate(taken, axis=0).astype(BF16)
            return carry

        lax.fori_loop(0, 128 // 16, gather_send, 0)
    face_copies = []
    for side, there in ((0, before_id), (1, after_id)):
        copy = pltpu.make_async_remote_copy(
            src_ref=fsend.at[side],
            dst_ref=frecv.at[1 - side],
            send_sem=fsend_sem.at[side],
            recv_sem=frecv_sem.at[1 - side],
            device_id=there,
            device_id_type=MESH,
        )
        copy.start()
        face_copies.append(copy)

    orow = iota((48, 1), 0)
    orow_v = div15(orow)
    orow_b = orow - NF * orow_v
    opick_v = onehot(orow_v == iota((48, NO), 1), F32)
    opick_b = onehot(orow_b == iota((48, NF), 1), F32)
    o_u = div5(lane)
    o_k = lane - NE * o_u
    o_ok = o_u < NO
    osel_k = onehot((o_k == iota((NE, 128), 0)) & o_ok, F32)
    osel_u = onehot((o_u == iota((NO, 128), 0)) & o_ok, F32)
    loads["ocean"].wait()
    loads["eproj"].wait()
    loads["osend"].wait()
    for v in range(NO):
        ost[NF * v : NF * (v + 1), :] = ocean[v]
    ost[NO * NF :, :] = jnp.zeros((48 - NO * NF, OC), F32)
    eprojs = [eproj[:, g, :] for g in range(3)]
    for g in range(3):
        proj = dot(opick_b, dot_tn(eprojs[g], osel_k, HIGHEST), HIGHEST)
        proj = jnp.where((orow_v == o_u) & o_ok, proj, 0.0)
        oext[LEAD + g * OC : LEAD + (g + 1) * OC, :] = dot_tn(ost[...], proj, HIGHEST)
    for side in range(2):
        for j in range(OBF):
            osend[side, j : j + 1, :] = oext[pl.ds(osend_s[side, j] + LEAD, 1), :]
    ocean_copies = []
    for side, there in ((0, (dom_before, sub)), (1, (dom_after, sub))):
        copy = pltpu.make_async_remote_copy(
            src_ref=osend.at[side],
            dst_ref=orecv.at[1 - side],
            send_sem=osend_sem.at[side],
            recv_sem=orecv_sem.at[1 - side],
            device_id=there,
            device_id_type=MESH,
        )
        copy.start()
        ocean_copies.append(copy)

    loads["flift"].wait()
    flifts = flift[...].astype(F32)
    flifts = [flifts[:, f, :].astype(BF16) for f in range(4)]
    eye = onehot(iota((NV, NV), 0) == iota((NV, NV), 1), F32)
    sel_u = [onehot((h_u == iota((NV, MAIN), 0)) & h_ok) for h_u, h_j, h_ok in halves]
    sel_u = jnp.concatenate(sel_u, axis=1)
    sel_jj = jnp.concatenate(sel_j, axis=1)
    own = [None, None, None]
    mrest = jnp.zeros((ROWS, MAIN), F32)
    for f in range(4):
        normal = 0.5 * (eye - combine(stars, TET[f]))
        both = spread(pick_v, normal, sel_u) * dot(
            pick_b, dot_tn(flifts[f], sel_jj).astype(BF16)
        )
        mmat[:, f * MAIN : (f + 1) * MAIN] = both[:, :MAIN].astype(BF16)
        mrest = mrest + jnp.where(
            lax.shift_right_logical(lane, 5) == f, both[:, MAIN:], 0.0
        )
        through = dot_tn(flifts[f], fprojs[f])
        for d, factor in TET[f]:
            term = through * -factor
            own[d] = term if own[d] is None else own[d] + term
    mmat[:, 4 * MAIN :] = mrest.astype(BF16)
    last = iota((1, ROWS), 1)
    last_u = div35(last)
    last_c = last - NB * last_u
    sel_u4 = onehot(last_u == iota((NV, ROWS), 0))
    sel_c4 = onehot(last_c == iota((NB, ROWS), 0))
    total = jnp.zeros((ROWS, ROWS), F32)
    for d in range(3):
        total = total + spread(pick_v, stars[d], sel_u4) * spread(pick_b, own[d], sel_c4)
    wmat[:, 3 * ROWS :] = total.astype(BF16)
    for cols in chunks:
        scaled(xs[3 * ROWS :, cols].astype(F32), cols)
    for cols in chunks:
        accf[:, cols] = xf[:, cols] + dot(wmat[...], xs[:, cols])

    loads["arrival"].wait()
    wide = iota((1, 1024), 1)
    wide_l = wide & 127
    wide_q = lax.shift_right_logical(wide, 7)
    pick_a = onehot(iota((128, 1), 0) == 8 * (wide_l & 15) + wide_q)
    targets = dot(arrival[...].astype(F32).astype(BF16), pick_a)
    targets = jnp.where(
        iota((8, 1), 0) == lax.shift_right_logical(wide_l, 4), targets, 0.0
    )
    targets = jnp.sum(targets, axis=0, keepdims=True)
    cells = iota((OC, 1), 0).astype(F32)
    pltpu.make_async_copy(
        arecv.at[pl.ds(0, N_DOM - 1)], arecv.at[pl.ds(0, N_DOM - 1)], arecv_sem
    ).wait()
    for s in range(N_DOM):
        pack[2 * s : 2 * s + 2, :] = arecv[s]
    arrived = pack[...].astype(BF16)
    forced = jnp.zeros((OC, 128), F32)
    for p in range(8):
        hits = onehot(targets[:, p * 128 : (p + 1) * 128] == cells)
        forced = forced + jnp.where(
            lax.shift_right_logical(lane, 4) == p, dot(hits, arrived), 0.0
        )
    fold = onehot((lane & 15) == iota((16, 128), 0), F32)
    part[sub] = dot_nt(fold, forced, HIGHEST)
    part_copies = []
    for k in range(1, N_SUB):
        copy = pltpu.make_async_remote_copy(
            src_ref=part.at[sub],
            dst_ref=part.at[sub],
            send_sem=psend_sem.at[k - 1],
            recv_sem=precv_sem.at[k - 1],
            device_id=(dom, lax.rem(sub + k, N_SUB)),
            device_id_type=MESH,
        )
        copy.start()
        part_copies.append(copy)

    for copy in face_copies:
        copy.wait_recv()
    has_before = (block > 0).astype(F32)
    has_after = (block < n_blocks - 1).astype(F32)
    for half in range(2):
        first = half * REST + LEAD + 4 * E
        ext[first : first + BF, :] = frecv[0, half].astype(F32) * has_before
        ext[first + BF : first + 2 * BF, :] = frecv[1, half].astype(F32) * has_after

    loads["nbr_s"].wait()
    face_lane = lax.shift_right_logical(iota((8, 128), 1), 5)

    def gather_block(block8, carry):
        def gather(i, carry):
            rests = []
            mains = [[], [], [], []]
            near_first = block8 * 512 + i * 16
            for h in range(2):
                e = pl.multiple_of(block8 * 128 + i * 16 + 8 * h, 8)
                rest = None
                for f in range(4):
                    slots8 = [nbr_s[near_first + (f * 128 + 8 * h + n)] for n in range(8)]
                    own_row = LEAD + f * E + e
                    mains[f].append(
                        rows8(ext, slots8) - ext[pl.ds(pl.multiple_of(own_row, 8), 8), :]
                    )
                    own_row = pl.multiple_of(own_row + REST, 8)
                    jump = rows8(ext, slots8, LEAD + REST) - ext[pl.ds(own_row, 8), :]
                    rest = jump if f == 0 else jnp.where(face_lane == f, jump, rest)
                rests.append(rest)
            rows = pl.ds(pl.multiple_of(block8 * 128 + i * 16, 16), 16)
            for f in range(4):
                jm[rows, f * MAIN : (f + 1) * MAIN] = jnp.concatenate(
                    mains[f], axis=0
                ).astype(BF16)
            jm[rows, 4 * MAIN :] = jnp.concatenate(rests, axis=0).astype(BF16)
            return carry

        return lax.fori_loop(0, 128 // 16, gather, carry)

    lax.fori_loop(0, E // 128, gather_block, 0)

    loads["fault"].wait()
    loads["fault_s"].wait()
    loads["strength"].wait()

    def gather_fault(i, carry):
        first = pl.multiple_of(i * 8, 8)
        near = [fault_s[first + n] for n in range(8)]
        far = [
            nbr_s[
                jnp.bitwise_and(lax.shift_right_logical(slot, 7), 7) * 512
                + lax.shift_right_logical(slot, 10) * 128
                + jnp.bitwise_and(slot, 127)
            ]
            for slot in near
        ]
        rows = pl.ds(first, 8)
        fjump[rows, :] = rows8(ext, far) - rows8(ext, near)
        fjump_rest[rows, :] = rows8(ext, far, LEAD + REST) - rows8(ext, near, LEAD + REST)
        return carry

    lax.fori_loop(0, 128 // 8, gather_fault, 0)
    limit = jnp.transpose(jnp.broadcast_to(strength[...], (128, 128)))
    faults = jnp.transpose(jnp.broadcast_to(fault[...].astype(F32), (128, 128)))
    faults = faults.astype(jnp.int32)
    fault_face = lax.shift_right_logical(faults, 10)
    inverse = 1.0 / limit
    change = limit * jnp.tanh(fjump[...] * inverse) - fjump[...]
    change_rest = limit * jnp.tanh(fjump_rest[...] * inverse) - fjump_rest[...]
    changes = [jnp.where(fault_face == f, change, 0.0) for f in range(4)]
    changes.append(
        jnp.where(fault_face == lax.shift_right_logical(lane, 5), change_rest, 0.0)
    )
    changes = jnp.concatenate(changes, axis=1).astype(BF16)
    lifted = dot_nt(mmat[...], changes).astype(BF16)
    fault_elem = (faults & (E - 1))[:, :1]

    out_copies = []
    for c, cols in enumerate(chunks):
        at = onehot(fault_elem == iota((1, CHUNK), 1) + c * CHUNK)
        accf[:, cols] = accf[:, cols] + dot_nt(mmat[...], jm[cols, :]) + dot(lifted, at)
        for v in range(NV):
            out_e[v, :, cols] = accf[NB * v : NB * (v + 1), cols].astype(BF16)
        copy = pltpu.make_async_copy(
            out_e.at[:, :, cols], out_e_h.at[:, :, cols], out_sem.at[c]
        )
        copy.start()
        out_copies.append(copy)

    loads["onbr"].wait()
    loads["okern"].wait()
    loads["shal"].wait()
    loads["elift"].wait()
    for side in range(2):
        ocean_copies[side].wait_recv()
    first = LEAD + 3 * OC
    oext[first : first + OBF, :] = orecv[0] * (dom > 0).astype(F32)
    oext[first + OBF : first + 2 * OBF, :] = orecv[1] * (dom < N_DOM - 1).astype(F32)

    for part_ in range(OC // 128):

        def ocean_gather(i, carry):
            for g in range(3):
                slots8 = [onbr_s[part_, g, i * 8 + n] for n in range(8)]
                rows = pl.ds(pl.multiple_of(g * OC + part_ * 128 + i * 8, 8), 8)
                obeside[rows, :] = rows8(oext, slots8)
            return carry

        lax.fori_loop(0, 128 // 8, ocean_gather, 0)
    shals = [shal[:, d, :] for d in range(2)]
    elifts = [elift[:, g, :] for g in range(3)]
    oeye = onehot(iota((NO, NO), 0) == iota((NO, NO), 1), F32)
    inner = [okern[:, d, :] for d in range(2)]
    updated = ost[...]
    for g in range(3):
        through = dot_tn(elifts[g], eprojs[g], HIGHEST)
        for d, factor in TRI[g]:
            inner[d] = inner[d] - factor * through
        normal = 0.25 * (oeye - combine(shals, TRI[g]))
        outer = dot(opick_v, dot(normal, osel_u, HIGHEST), HIGHEST)
        lifts = dot(opick_b, dot_tn(elifts[g], osel_k, HIGHEST), HIGHEST)
        ojump = obeside[g * OC : (g + 1) * OC, :] - oext[LEAD + g * OC : LEAD + (g + 1) * OC, :]
        updated = updated + dot_nt(outer * lifts, ojump, HIGHEST)
    volume = jnp.zeros((48, 48), F32)
    for d in range(2):
        left = dot_nt(dot(opick_v, shals[d], HIGHEST), opick_v, HIGHEST)
        right = dot_nt(dot(opick_b, inner[d], HIGHEST), opick_b, HIGHEST)
        volume = volume + left * right
    oacc[...] = updated + 0.5 * dot(volume, ost[...], HIGHEST)

    for copy in part_copies:
        copy.wait_recv()
    oacc[:16, :] = oacc[:16, :] + (part[0] + part[1] + part[2] + part[3])
    for v in range(NO):
        out_o[v] = oacc[NF * v : NF * (v + 1), :]
    copy = pltpu.make_async_copy(out_o, out_o_h, out_sem.at[E // CHUNK])
    copy.start()
    out_copies.append(copy)

    for copy in face_copies + ocean_copies + part_copies:
        copy.wait_send()
    pltpu.make_async_copy(
        asend.at[pl.ds(0, N_DOM - 1)], asend.at[pl.ds(0, N_DOM - 1)], asend_sem
    ).wait()
    for copy in out_copies:
        copy.wait()


def place_kernel(elastic, ocean, out_e, out_o, held, held_o, in_sem, out_sem):
    arriving = [
        pltpu.make_async_copy(elastic.at[v], held.at[v], in_sem.at[v]) for v in range(NV)
    ]
    arriving.append(pltpu.make_async_copy(ocean, held_o, in_sem.at[NV]))
    leaving = [
        pltpu.make_async_copy(held.at[v], out_e.at[v], out_sem.at[v]) for v in range(NV)
    ]
    leaving.append(pltpu.make_async_copy(held_o, out_o, out_sem.at[NV]))
    for copy in arriving:
        copy.start()
    for first, second in zip(arriving, leaving):
        first.wait()
        second.start()
    for copy in leaving:
        copy.wait()


def lane_blocks(indices):
    rows, columns = indices.shape
    return jnp.transpose(indices.reshape(rows, columns // 128, 128), (1, 0, 2))


def body(
    elastic,
    jacobian,
    star_mats,
    stiffness,
    face_proj,
    face_lift,
    clusters,
    neighbours,
    send_faces,
    fault_faces,
    fault_strength,
    seafloor_faces,
    seafloor_slots,
    arrival_cells,
    ocean_state,
    ocean_kernels,
    shallow_mats,
    edge_proj,
    edge_lift,
    ocean_send,
    ocean_neighbours,
):
    anywhere = pl.BlockSpec(memory_space=pl.ANY)
    dma = pltpu.SemaphoreType.DMA
    I32 = jnp.int32
    inputs = (
        elastic,
        jacobian,
        jnp.transpose(star_mats, (1, 0, 2)),
        stiffness,
        jnp.transpose(face_proj, (1, 0, 2)),
        jnp.transpose(face_lift, (2, 0, 1)),
        clusters.reshape(1, E),
        lane_blocks(neighbours).reshape(-1),
        lane_blocks(send_faces).reshape(-1),
        fault_faces.reshape(1, 128),
        fault_strength.reshape(1, 128),
        seafloor_faces,
        seafloor_slots.reshape(1, 512),
        arrival_cells.reshape(8, 128),
        ocean_state,
        jnp.transpose(ocean_kernels, (1, 0, 2)),
        jnp.transpose(shallow_mats, (1, 0, 2)),
        jnp.transpose(edge_proj, (1, 0, 2)),
        jnp.transpose(edge_lift, (2, 0, 1)),
        ocean_send,
        lane_blocks(ocean_neighbours),
        fault_faces,
    )
    results = pl.pallas_call(
        main_kernel,
        out_shape=(
            jax.ShapeDtypeStruct(elastic.shape, BF16),
            jax.ShapeDtypeStruct(ocean_state.shape, F32),
        ),
        in_specs=[anywhere] * len(inputs),
        out_specs=(anywhere, anywhere),
        scratch_shapes=[
            pltpu.VMEM((NV, NB, E), BF16),
            pltpu.VMEM((3, E), F32),
            pltpu.VMEM((NV, 3, NV), F32),
            pltpu.VMEM((3, NB, NB), BF16),
            pltpu.VMEM((NF, 4, NB), BF16),
            pltpu.VMEM((NF, 4, NB), BF16),
            pltpu.VMEM((1, E), I32),
            pltpu.SMEM((4 * E,), I32),
            pltpu.SMEM((2 * BF,), I32),
            pltpu.VMEM((1, 128), I32),
            pltpu.SMEM((128,), I32),
            pltpu.VMEM((1, 128), F32),
            pltpu.SMEM((512,), I32),
            pltpu.VMEM((1, 512), I32),
            pltpu.VMEM((8, 128), I32),
            pltpu.VMEM((NO, NF, OC), F32),
            pltpu.VMEM((NF, 2, NF), F32),
            pltpu.VMEM((NO, 2, NO), F32),
            pltpu.VMEM((NE, 3, NF), F32),
            pltpu.VMEM((NE, 3, NF), F32),
            pltpu.SMEM((2, OBF), I32),
            pltpu.SMEM((OC // 128, 3, 128), I32),
            dma((22,)),
            pltpu.VMEM((ROWS, E), F32),
            pltpu.VMEM((4 * ROWS, E), BF16),
            pltpu.VMEM((ROWS, 4 * ROWS), BF16),
            pltpu.VMEM((ROWS, 8 * MAIN), BF16),
            pltpu.VMEM((ROWS, 5 * MAIN), BF16),
            pltpu.VMEM((ROWS, E), F32),
            pltpu.VMEM((2 * REST, MAIN), F32),
            pltpu.VMEM((E, 5 * MAIN), BF16),
            pltpu.VMEM((128, MAIN), F32),
            pltpu.VMEM((128, MAIN), F32),
            pltpu.VMEM((2, 2, BF, MAIN), BF16),
            pltpu.VMEM((2, 2, BF, MAIN), BF16),
            pltpu.VMEM((NV, NB, E), BF16),
            pltpu.VMEM((NO, NF, OC), F32),
            pltpu.VMEM((48, OC), F32),
            pltpu.VMEM((3 * OC + 2 * OBF + 2 * LEAD, 128), F32),
            pltpu.VMEM((3 * OC, 128), F32),
            pltpu.VMEM((2, OBF, 128), F32),
            pltpu.VMEM((2, OBF, 128), F32),
            pltpu.VMEM((48, OC), F32),
            pltpu.VMEM((512, 128), F32),
            pltpu.VMEM((128, 128), F32),
            pltpu.VMEM((N_DOM, 2, 128), F32),
            pltpu.VMEM((N_DOM, 2, 128), F32),
            pltpu.VMEM((N_SUB, 16, OC), F32),
            dma((2,)),
            dma((2,)),
            dma((2,)),
            dma((2,)),
            dma,
            dma,
            dma((3,)),
            dma((3,)),
            dma((E // CHUNK + 1,)),
        ],
        compiler_params=pltpu.CompilerParams(
            collective_id=0,
            has_side_effects=True,
            vmem_limit_bytes=60 * 1024 * 1024,
        ),
    )(*inputs)
    return pl.pallas_call(
        place_kernel,
        out_shape=(
            jax.ShapeDtypeStruct(elastic.shape, BF16),
            jax.ShapeDtypeStruct(ocean_state.shape, F32),
        ),
        in_specs=[anywhere] * 2,
        out_specs=(anywhere, anywhere),
        scratch_shapes=[
            pltpu.VMEM((NV, NB, E), BF16),
            pltpu.VMEM((NO, NF, OC), F32),
            dma((NV + 1,)),
            dma((NV + 1,)),
        ],
        compiler_params=pltpu.CompilerParams(vmem_limit_bytes=60 * 1024 * 1024),
    )(*results)


def solution(mesh):
    both = ("dom", "sub")
    return jax.shard_map(
        body,
        mesh=mesh,
        in_specs=(
            P(None, None, both),
            P(None, both),
            P(),
            P(),
            P(),
            P(),
            P(both),
            P(None, both),
            P(None, both),
            P(both),
            P(both),
            P(both),
            P(both),
            P(both),
            P(None, None, "dom"),
            P(),
            P(),
            P(),
            P(),
            P(None, "dom"),
            P(None, "dom"),
        ),
        out_specs=(P(None, None, both), P(None, None, "dom")),
        check_vma=False,
    )
```

```python
import functools

import jax
import jax.numpy as jnp
from jax import lax
from jax.experimental import pallas as pl
from jax.experimental.pallas import tpu as pltpu
from jax.sharding import PartitionSpec as P

MESH = pl.DeviceIdType.MESH
F32, BF16 = jnp.float32, jnp.bfloat16

NV, NB, NF = 9, 35, 15
NO, NE = 3, 5
ROWS = 320
WIDE = 384
E = 1024
BF = 256
OC, OBF = 256, 32
CAP = 16
N_DOM, N_SUB = 64, 4
CHUNK = 256
MAIN = 128
LEAD = 8
REST = 4 * E + 2 * BF + 2 * LEAD
ROOT3 = 0.57735027
ROOT2 = 0.70710678
TET = [
    [(2, -1.0)],
    [(1, -1.0)],
    [(0, -1.0)],
    [(0, ROOT3), (1, ROOT3), (2, ROOT3)],
]
TRI = [[(1, -1.0)], [(0, -1.0)], [(0, ROOT2), (1, ROOT2)]]


def iota(shape, dim):
    return lax.broadcasted_iota(jnp.int32, shape, dim)


def div35(x):
    return lax.shift_right_logical(x * 1873, 16)


def div15(x):
    return lax.shift_right_logical(x * 4370, 16)


def div5(x):
    return lax.shift_right_logical(x * 13108, 16)


def onehot(cond, dtype=BF16):
    return jnp.where(cond, 1.0, 0.0).astype(dtype)


def dot(a, b):
    return lax.dot_general(
        a.astype(BF16), b.astype(BF16), (((1,), (0,)), ((), ())), preferred_element_type=F32
    )


def dot_tn(a, b):
    return lax.dot_general(
        a.astype(BF16), b.astype(BF16), (((0,), (0,)), ((), ())), preferred_element_type=F32
    )


def dot_nt(a, b):
    return lax.dot_general(
        a.astype(BF16), b.astype(BF16), (((1,), (1,)), ((), ())), preferred_element_type=F32
    )


def combine(mats, pairs):
    total = None
    for direction, factor in pairs:
        term = mats[direction] * factor
        total = term if total is None else total + term
    return total


def spread(select_rows, mat, select_cols):
    return dot(select_rows, dot(mat.astype(BF16), select_cols).astype(BF16))


def face_columns(q):
    group = div15(q)
    variable = jnp.where(group == 0, NV - 1, group - 1)
    return variable, q - NF * group, group < NV


def main_kernel(
    elastic_h,
    jac_h,
    star_h,
    stiff_h,
    fproj_h,
    flift_h,
    clusters_h,
    nbr_h,
    send_h,
    fault_h,
    strength_h,
    floor_h,
    slots_h,
    arrival_h,
    ocean_h,
    okern_h,
    shal_h,
    eproj_h,
    elift_h,
    osend_h,
    onbr_h,
    fault1_h,
    out_e_h,
    out_o_h,
    elastic,
    jac,
    star,
    stiff,
    fproj,
    flift,
    clusters,
    nbr_s,
    send_s,
    fault,
    fault_s,
    strength,
    floor_s,
    slots,
    arrival,
    ocean,
    okern,
    shal,
    eproj,
    elift,
    osend_s,
    onbr_s,
    in_sem,
    step,
    xf,
    xs,
    wmat,
    fmat,
    mmat,
    accf,
    ext,
    jm,
    fjump,
    fjump_rest,
    fsend,
    frecv,
    out_e,
    out_o,
    oacc,
    oext,
    obeside,
    osend,
    orecv,
    ost,
    upl,
    pack,
    asend,
    arecv,
    part,
    fsend_sem,
    frecv_sem,
    osend_sem,
    orecv_sem,
    asend_sem,
    arecv_sem,
    psend_sem,
    precv_sem,
    out_sem,
):
    loads = {}
    pairs = (
        ("star", star_h, star),
        ("stiff", stiff_h, stiff),
        ("elastic", elastic_h, elastic),
        ("jac", jac_h, jac),
        ("clusters", clusters_h, clusters),
        ("fproj", fproj_h, fproj),
        ("floor", floor_h, floor_s),
        ("slots", slots_h, slots),
        ("send_s", send_h, send_s),
        ("nbr_s", nbr_h, nbr_s),
        ("flift", flift_h, flift),
        ("arrival", arrival_h, arrival),
        ("fault", fault_h, fault),
        ("fault_s", fault1_h, fault_s),
        ("strength", strength_h, strength),
        ("ocean", ocean_h, ocean),
        ("eproj", eproj_h, eproj),
        ("osend", osend_h, osend_s),
        ("onbr", onbr_h, onbr_s),
        ("okern", okern_h, okern),
        ("shal", shal_h, shal),
        ("elift", elift_h, elift),
    )
    for n, (name, source, target) in enumerate(pairs):
        loads[name] = pltpu.make_async_copy(source, target, in_sem.at[n])
        loads[name].start()

    dom = lax.axis_index("dom")
    sub = lax.axis_index("sub")
    block = dom * N_SUB + sub
    n_blocks = N_DOM * N_SUB
    after = lax.rem(block + 1, n_blocks)
    before = lax.rem(block + n_blocks - 1, n_blocks)
    after_id = (lax.div(after, N_SUB), lax.rem(after, N_SUB))
    before_id = (lax.div(before, N_SUB), lax.rem(before, N_SUB))
    dom_after = lax.rem(dom + 1, N_DOM)
    dom_before = lax.rem(dom + N_DOM - 1, N_DOM)

    barrier = pltpu.get_barrier_semaphore()

    def greet(i, carry):
        for k in range(1, 10):
            there = (lax.rem(dom + i * 9 + k, N_DOM), sub)
            pl.semaphore_signal(barrier, inc=1, device_id=there, device_id_type=MESH)
        return carry

    lax.fori_loop(0, 7, greet, 0)
    for k in range(1, N_SUB):
        there = (dom, lax.rem(sub + k, N_SUB))
        pl.semaphore_signal(barrier, inc=1, device_id=there, device_id_type=MESH)
    for there in (before_id, after_id):
        pl.semaphore_signal(barrier, inc=1, device_id=there, device_id_type=MESH)

    row = iota((ROWS, 1), 0)
    row_v = div35(row)
    row_b = row - NB * row_v
    pick_v = onehot(row_v == iota((ROWS, NV), 1))
    pick_b = onehot(row_b == iota((ROWS, NB), 1))

    col = iota((1, 3 * ROWS), 1)
    col_d = (col >= ROWS).astype(jnp.int32) + (col >= 2 * ROWS).astype(jnp.int32)
    col_r = col - ROWS * col_d
    col_u = div35(col_r)
    col_c = col_r - NB * col_u
    loads["star"].wait()
    loads["stiff"].wait()
    stars = [star[:, d, :] for d in range(3)]
    a_cols, k_cols = None, None
    for d in range(3):
        sel_u = onehot((col_d == d) & (col_u == iota((NV, 3 * ROWS), 0)))
        sel_c = onehot((col_d == d) & (col_c == iota((NB, 3 * ROWS), 0)))
        terms = (dot(stars[d].astype(BF16), sel_u), dot(stiff[d], sel_c))
        if d == 0:
            a_cols, k_cols = terms
        else:
            a_cols, k_cols = a_cols + terms[0], k_cols + terms[1]
    wmat[:, : 3 * ROWS] = (
        dot(pick_v, a_cols.astype(BF16)) * dot(pick_b, k_cols.astype(BF16))
    ).astype(BF16)

    loads["elastic"].wait()
    for v in range(NV):
        xf[NB * v : NB * (v + 1), :] = elastic[v].astype(F32)
    xf[NV * NB :, :] = jnp.zeros((ROWS - NV * NB, E), F32)
    loads["jac"].wait()
    loads["clusters"].wait()
    step[...] = 0.5 * jnp.exp2(-clusters[...].astype(F32))
    chunks = [slice(c * CHUNK, (c + 1) * CHUNK) for c in range(E // CHUNK)]

    def scaled(x, cols):
        for d in range(3):
            xs[d * ROWS : (d + 1) * ROWS, cols] = (jac[d : d + 1, cols] * x).astype(BF16)

    for cols in chunks:
        scaled(xf[:, cols], cols)

    loads["fproj"].wait()
    fprojs = fproj[...].astype(F32)
    fprojs = [fprojs[:, f, :].astype(BF16) for f in range(4)]
    lane = iota((1, 128), 1)
    q_u, q_j, q_ok = face_columns(lane)
    r_lane = lane & 31
    r_u, r_j, r_ok = face_columns(MAIN + r_lane)
    r_ok = r_ok & (r_lane < 8)
    halves = ((q_u, q_j, q_ok), (r_u, r_j, r_ok))
    sel_j = [onehot((h_j == iota((NF, MAIN), 0)) & h_ok) for h_u, h_j, h_ok in halves]
    for half, (h_u, h_j, h_ok) in enumerate(halves):
        pair_u = jnp.concatenate([jnp.where(h_ok, h_u, -1)] * 2, axis=1)
        for f in range(0, 4, 2):
            proj = [dot_tn(fprojs[f + n], sel_j[half]).astype(BF16) for n in range(2)]
            proj = dot(pick_b, jnp.concatenate(proj, axis=1))
            fmat[:, (4 * half + f) * MAIN : (4 * half + f + 2) * MAIN] = jnp.where(
                row_v == pair_u, proj, 0.0
            ).astype(BF16)

    for cols in chunks:
        h = step[:, cols]
        term = dot(wmat[:, : 3 * ROWS], xs[: 3 * ROWS, cols])
        accf[:, cols] = h * xf[:, cols] + (h * h * 0.5) * term
        scaled(term, cols)
    for cols in chunks:
        h = step[:, cols]
        term = dot(wmat[:, : 3 * ROWS], xs[: 3 * ROWS, cols])
        integral = (accf[:, cols] + (h * h * h * (1.0 / 6.0)) * term).astype(BF16)
        xs[3 * ROWS :, cols] = integral
    for c, cols in enumerate(chunks):
        traced = dot_tn(xs[3 * ROWS :, cols], fmat[...])
        for f in range(4):
            rows = slice(LEAD + f * E + c * CHUNK, LEAD + f * E + (c + 1) * CHUNK)
            ext[rows, :] = traced[:, f * MAIN : (f + 1) * MAIN]
            rows = slice(REST + rows.start, REST + rows.stop)
            ext[rows, :] = traced[:, (4 + f) * MAIN : (5 + f) * MAIN]

    sublane = iota((8, 128), 0)

    def rows8(table, slots8, start=LEAD):
        taken = None
        for k in range(8):
            row = jnp.broadcast_to(table[pl.ds(slots8[k] + start, 1), :], (8, 128))
            taken = row if k == 0 else jnp.where(sublane == k, row, taken)
        return taken

    loads["floor"].wait()
    loads["slots"].wait()
    loads["send_s"].wait()

    def gather_floor(i, carry):
        for k in range(4):
            first = pl.multiple_of(i * 32 + 8 * k, 8)
            upl[pl.ds(first, 8), :] = rows8(ext, [floor_s[first + n] for n in range(8)])
        return carry

    lax.fori_loop(0, 512 // 32, gather_floor, 0)
    moved = jnp.where(lane < NF, upl[...], 0.0)
    for shift in (16, 32, 64):
        moved = moved + pltpu.roll(moved, shift, 1)
    moved = moved.astype(BF16)
    places = iota((128, 1), 0) * 8
    packed = jnp.zeros((128, 128), F32)
    for p in range(8):
        hits = onehot(slots[...] == places + p)
        packed = packed + jnp.where(
            lax.shift_right_logical(lane, 4) == p, dot(hits, moved), 0.0
        )
    pack[...] = packed
    for d in range(N_DOM):
        asend[d] = pack[2 * d : 2 * d + 2, :]
    arecv[dom] = asend[dom]

    pl.semaphore_wait(barrier, N_DOM - 1 + N_SUB - 1 + 2)

    def send_floor(i, carry):
        for k in range(1, 10):
            there = lax.rem(dom + i * 9 + k, N_DOM)
            pltpu.make_async_remote_copy(
                src_ref=asend.at[there],
                dst_ref=arecv.at[dom],
                send_sem=asend_sem,
                recv_sem=arecv_sem,
                device_id=(there, sub),
                device_id_type=MESH,
            ).start()
        return carry

    lax.fori_loop(0, 7, send_floor, 0)

    for part_ in range(BF // 128):

        def gather_send(i, carry):
            first = pl.multiple_of(i * 16, 16)
            for side in range(2):
                slots = [send_s[part_ * 256 + side * 128 + first + n] for n in range(16)]
                taken = [rows8(ext, slots[8 * h : 8 * h + 8]) for h in range(2)]
                rows = pl.ds(part_ * 128 + first, 16)
                fsend[side, rows, :] = jnp.concatenate(taken, axis=0).astype(BF16)
            return carry

        lax.fori_loop(0, 128 // 16, gather_send, 0)
    face_lane = lax.shift_right_logical(iota((8, 128), 1), 5)

    def gather_send_rest(i, carry):
        first = pl.multiple_of(i * 16, 16)
        for side in range(2):
            packed = []
            for h in range(2):
                whole = None
                for g in range(4):
                    at = (g // 2) * 256 + side * 128 + (g % 2) * 64 + 8 * h
                    slots8 = [send_s[first + (at + n)] for n in range(8)]
                    taken = rows8(ext, slots8, LEAD + REST)
                    whole = taken if g == 0 else jnp.where(face_lane == g, taken, whole)
                packed.append(whole)
            rows = pl.ds(BF + first, 16)
            fsend[side, rows, :] = jnp.concatenate(packed, axis=0).astype(BF16)
        return carry

    lax.fori_loop(0, 64 // 16, gather_send_rest, 0)
    face_copies = []
    for side, there in ((0, before_id), (1, after_id)):
        copy = pltpu.make_async_remote_copy(
            src_ref=fsend.at[side],
            dst_ref=frecv.at[1 - side],
            send_sem=fsend_sem.at[side],
            recv_sem=frecv_sem.at[1 - side],
            device_id=there,
            device_id_type=MESH,
        )
        copy.start()
        face_copies.append(copy)

    orow = iota((48, 1), 0)
    orow_v = div15(orow)
    orow_b = orow - NF * orow_v
    opick_v = onehot(orow_v == iota((48, NO), 1), F32)
    opick_b = onehot(orow_b == iota((48, NF), 1), F32)
    o_u = div5(lane)
    o_k = lane - NE * o_u
    o_ok = o_u < NO
    osel_k = onehot((o_k == iota((NE, 128), 0)) & o_ok, F32)
    osel_u = onehot((o_u == iota((NO, 128), 0)) & o_ok, F32)
    loads["ocean"].wait()
    loads["eproj"].wait()
    loads["osend"].wait()
    for v in range(NO):
        ost[NF * v : NF * (v + 1), :] = ocean[v]
    ost[NO * NF :, :] = jnp.zeros((48 - NO * NF, OC), F32)
    eprojs = [eproj[:, g, :] for g in range(3)]
    for g in range(3):
        proj = dot(opick_b, dot_tn(eprojs[g], osel_k))
        proj = jnp.where((orow_v == o_u) & o_ok, proj, 0.0)
        oext[LEAD + g * OC : LEAD + (g + 1) * OC, :] = dot_tn(ost[...], proj)
    for side in range(2):
        for j in range(OBF):
            osend[side, j : j + 1, :] = oext[pl.ds(osend_s[side, j] + LEAD, 1), :]
    ocean_copies = []
    for side, there in ((0, (dom_before, sub)), (1, (dom_after, sub))):
        copy = pltpu.make_async_remote_copy(
            src_ref=osend.at[side],
            dst_ref=orecv.at[1 - side],
            send_sem=osend_sem.at[side],
            recv_sem=orecv_sem.at[1 - side],
            device_id=there,
            device_id_type=MESH,
        )
        copy.start()
        ocean_copies.append(copy)

    loads["flift"].wait()
    flifts = flift[...].astype(F32)
    flifts = [flifts[:, f, :].astype(BF16) for f in range(4)]
    eye = onehot(iota((NV, NV), 0) == iota((NV, NV), 1), F32)
    last = iota((1, WIDE), 1)
    last_u = div35(last)
    last_c = last - NB * last_u
    wide_u = onehot(last_u == iota((NV, WIDE), 0))
    wide_c = onehot(last_c == iota((NB, WIDE), 0))
    down = iota((2 * MAIN, 1), 0)
    down_lane = down & (MAIN - 1)
    down_r = down_lane & 31
    down_q = jnp.where(down < MAIN, down_lane, MAIN + down_r)
    down_u, down_j, down_ok = face_columns(down_q)
    down_ok = down_ok & ((down < MAIN) | (down_r < 8))
    down_u = onehot((down_u == iota((2 * MAIN, NV), 1)) & down_ok)
    down_j = onehot((down_j == iota((2 * MAIN, NF), 1)) & down_ok)
    down_face = lax.shift_right_logical(down_lane[MAIN:], 5)
    own = [None, None, None]
    mrest = jnp.zeros((MAIN, WIDE), F32)
    for f in range(4):
        normal = 0.5 * (eye - combine(stars, TET[f]))
        both = dot(down_u, dot_tn(normal, wide_u)) * dot(
            down_j, dot(flifts[f], wide_c)
        )
        mmat[f * MAIN : (f + 1) * MAIN, :] = both[:MAIN].astype(BF16)
        mrest = mrest + jnp.where(down_face == f, both[MAIN:], 0.0)
        through = dot_tn(flifts[f], fprojs[f])
        for d, factor in TET[f]:
            term = through * -factor
            own[d] = term if own[d] is None else own[d] + term
    mmat[4 * MAIN : 5 * MAIN, :] = mrest.astype(BF16)
    sel_u4 = wide_u[:, :ROWS]
    sel_c4 = wide_c[:, :ROWS]
    total = jnp.zeros((ROWS, ROWS), F32)
    for d in range(3):
        total = total + spread(pick_v, stars[d], sel_u4) * spread(pick_b, own[d], sel_c4)
    wmat[:, 3 * ROWS :] = total.astype(BF16)
    for cols in chunks:
        scaled(xs[3 * ROWS :, cols].astype(F32), cols)
    for cols in chunks:
        accf[:, cols] = xf[:, cols] + dot(wmat[...], xs[:, cols])

    loads["onbr"].wait()
    loads["okern"].wait()
    loads["shal"].wait()
    loads["elift"].wait()
    for side in range(2):
        ocean_copies[side].wait_recv()
    first = LEAD + 3 * OC
    oext[first : first + OBF, :] = orecv[0] * (dom > 0).astype(F32)
    oext[first + OBF : first + 2 * OBF, :] = orecv[1] * (dom < N_DOM - 1).astype(F32)

    for part_ in range(OC // 128):

        def ocean_gather(i, carry):
            for g in range(3):
                slots8 = [onbr_s[part_, g, i * 8 + n] for n in range(8)]
                rows = pl.ds(pl.multiple_of(g * OC + part_ * 128 + i * 8, 8), 8)
                obeside[rows, :] = rows8(oext, slots8)
            return carry

        lax.fori_loop(0, 128 // 8, ocean_gather, 0)
    shals = [shal[:, d, :] for d in range(2)]
    elifts = [elift[:, g, :] for g in range(3)]
    oeye = onehot(iota((NO, NO), 0) == iota((NO, NO), 1), F32)
    inner = [okern[:, d, :] for d in range(2)]
    updated = ost[...]
    for g in range(3):
        through = dot_tn(elifts[g], eprojs[g])
        for d, factor in TRI[g]:
            inner[d] = inner[d] - factor * through
        normal = 0.25 * (oeye - combine(shals, TRI[g]))
        outer = dot(opick_v, dot(normal, osel_u))
        lifts = dot(opick_b, dot_tn(elifts[g], osel_k))
        ojump = obeside[g * OC : (g + 1) * OC, :] - oext[LEAD + g * OC : LEAD + (g + 1) * OC, :]
        updated = updated + dot_nt(outer * lifts, ojump)
    volume = jnp.zeros((48, 48), F32)
    for d in range(2):
        left = dot_nt(dot(opick_v, shals[d]), opick_v)
        right = dot_nt(dot(opick_b, inner[d]), opick_b)
        volume = volume + left * right
    oacc[...] = updated + 0.5 * dot(volume, ost[...])

    for copy in face_copies:
        copy.wait_recv()
    has_before = (block > 0).astype(F32)
    has_after = (block < n_blocks - 1).astype(F32)
    for side, keep in ((0, has_before), (1, has_after)):
        first = LEAD + 4 * E + side * BF
        ext[first : first + BF, :] = frecv[side, :BF, :].astype(F32) * keep
        packed = frecv[side, BF:, :].astype(F32) * keep
        for g in range(4):
            one = jnp.where(lax.shift_right_logical(lane, 5) == g, packed, 0.0)
            one = one + pltpu.roll(one, 32, 1)
            one = one + pltpu.roll(one, 64, 1)
            ext[REST + first + 64 * g : REST + first + 64 * (g + 1), :] = one

    loads["nbr_s"].wait()

    def gather_block(block8, carry):
        def gather(i, carry):
            rests = []
            mains = [[], [], [], []]
            near_first = block8 * 512 + i * 16
            for h in range(2):
                e = pl.multiple_of(block8 * 128 + i * 16 + 8 * h, 8)
                rest = None
                for f in range(4):
                    slots8 = [nbr_s[near_first + (f * 128 + 8 * h + n)] for n in range(8)]
                    own_row = LEAD + f * E + e
                    mains[f].append(
                        rows8(ext, slots8) - ext[pl.ds(pl.multiple_of(own_row, 8), 8), :]
                    )
                    own_row = pl.multiple_of(own_row + REST, 8)
                    jump = rows8(ext, slots8, LEAD + REST) - ext[pl.ds(own_row, 8), :]
                    rest = jump if f == 0 else jnp.where(face_lane == f, jump, rest)
                rests.append(rest)
            rows = pl.ds(pl.multiple_of(block8 * 128 + i * 16, 16), 16)
            for f in range(4):
                jm[rows, f * MAIN : (f + 1) * MAIN] = jnp.concatenate(
                    mains[f], axis=0
                ).astype(BF16)
            jm[rows, 4 * MAIN : 5 * MAIN] = jnp.concatenate(rests, axis=0).astype(BF16)
            return carry

        return lax.fori_loop(0, 128 // 16, gather, carry)

    lax.fori_loop(0, 1, gather_block, 0)

    loads["arrival"].wait()
    wide = iota((1, 1024), 1)
    wide_l = wide & 127
    wide_q = lax.shift_right_logical(wide, 7)
    pick_a = onehot(iota((128, 1), 0) == 8 * (wide_l & 15) + wide_q)
    targets = dot(arrival[...].astype(F32).astype(BF16), pick_a)
    targets = jnp.where(
        iota((8, 1), 0) == lax.shift_right_logical(wide_l, 4), targets, 0.0
    )
    targets = jnp.sum(targets, axis=0, keepdims=True)
    cells = iota((OC, 1), 0).astype(F32)
    pltpu.make_async_copy(
        arecv.at[pl.ds(0, N_DOM - 1)], arecv.at[pl.ds(0, N_DOM - 1)], arecv_sem
    ).wait()
    for s in range(N_DOM):
        pack[2 * s : 2 * s + 2, :] = arecv[s]
    arrived = pack[...].astype(BF16)
    forced = jnp.zeros((OC, 128), F32)
    for p in range(8):
        hits = onehot(targets[:, p * 128 : (p + 1) * 128] == cells)
        forced = forced + jnp.where(
            lax.shift_right_logical(lane, 4) == p, dot(hits, arrived), 0.0
        )
    fold = onehot((lane & 15) == iota((16, 128), 0), F32)
    part[sub] = dot_nt(fold, forced)
    part_copies = []
    for k in range(1, N_SUB):
        copy = pltpu.make_async_remote_copy(
            src_ref=part.at[sub],
            dst_ref=part.at[sub],
            send_sem=psend_sem.at[k - 1],
            recv_sem=precv_sem.at[k - 1],
            device_id=(dom, lax.rem(sub + k, N_SUB)),
            device_id_type=MESH,
        )
        copy.start()
        part_copies.append(copy)

    lax.fori_loop(1, E // 128, gather_block, 0)

    loads["fault"].wait()
    loads["fault_s"].wait()
    loads["strength"].wait()

    def gather_fault(i, carry):
        first = pl.multiple_of(i * 8, 8)
        near = [fault_s[first + n] for n in range(8)]
        far = [
            nbr_s[
                jnp.bitwise_and(lax.shift_right_logical(slot, 7), 7) * 512
                + lax.shift_right_logical(slot, 10) * 128
                + jnp.bitwise_and(slot, 127)
            ]
            for slot in near
        ]
        rows = pl.ds(first, 8)
        fjump[rows, :] = rows8(ext, far) - rows8(ext, near)
        fjump_rest[rows, :] = rows8(ext, far, LEAD + REST) - rows8(ext, near, LEAD + REST)
        return carry

    lax.fori_loop(0, 128 // 8, gather_fault, 0)
    limit = jnp.transpose(jnp.broadcast_to(strength[...], (128, 128)))
    faults = jnp.transpose(jnp.broadcast_to(fault[...].astype(F32), (128, 128)))
    faults = faults.astype(jnp.int32)
    fault_face = lax.shift_right_logical(faults, 10)
    inverse = 1.0 / limit
    change = limit * jnp.tanh(fjump[...] * inverse) - fjump[...]
    change_rest = limit * jnp.tanh(fjump_rest[...] * inverse) - fjump_rest[...]
    changes = [jnp.where(fault_face == f, change, 0.0) for f in range(4)]
    changes.append(
        jnp.where(fault_face == lax.shift_right_logical(lane, 5), change_rest, 0.0)
    )
    changes = jnp.concatenate(changes, axis=1).astype(BF16)
    mmat[5 * MAIN :, :] = dot(changes, mmat[: 5 * MAIN, :]).astype(BF16)
    fault_elem = fault[...] & (E - 1)
    jm[:, 5 * MAIN :] = onehot(fault_elem == iota((E, 1), 0))

    for cols in chunks:
        change = jnp.transpose(dot(jm[cols, :], mmat[...]))
        accf[:, cols] = accf[:, cols] + change[:ROWS]
    out_copies = []
    for v in range(NV):
        out_e[v] = accf[NB * v : NB * (v + 1), :].astype(BF16)
        copy = pltpu.make_async_copy(out_e.at[v], out_e_h.at[v], out_sem.at[v])
        copy.start()
        out_copies.append(copy)

    for copy in part_copies:
        copy.wait_recv()
    oacc[:16, :] = oacc[:16, :] + (part[0] + part[1] + part[2] + part[3])
    for v in range(NO):
        out_o[v] = oacc[NF * v : NF * (v + 1), :]
    copy = pltpu.make_async_copy(out_o, out_o_h, out_sem.at[NV])
    copy.start()
    out_copies.append(copy)

    for copy in face_copies + ocean_copies + part_copies:
        copy.wait_send()
    pltpu.make_async_copy(
        asend.at[pl.ds(0, N_DOM - 1)], asend.at[pl.ds(0, N_DOM - 1)], asend_sem
    ).wait()
    for copy in out_copies:
        copy.wait()


def place_kernel(elastic, ocean, out_e, out_o, held, held_o, in_sem, out_sem):
    arriving = [
        pltpu.make_async_copy(elastic.at[v], held.at[v], in_sem.at[v]) for v in range(NV)
    ]
    arriving.append(pltpu.make_async_copy(ocean, held_o, in_sem.at[NV]))
    leaving = [
        pltpu.make_async_copy(held.at[v], out_e.at[v], out_sem.at[v]) for v in range(NV)
    ]
    leaving.append(pltpu.make_async_copy(held_o, out_o, out_sem.at[NV]))
    for copy in arriving:
        copy.start()
    for first, second in zip(arriving, leaving):
        first.wait()
        second.start()
    for copy in leaving:
        copy.wait()


def lane_blocks(indices):
    rows, columns = indices.shape
    return jnp.transpose(indices.reshape(rows, columns // 128, 128), (1, 0, 2))


def body(
    elastic,
    jacobian,
    star_mats,
    stiffness,
    face_proj,
    face_lift,
    clusters,
    neighbours,
    send_faces,
    fault_faces,
    fault_strength,
    seafloor_faces,
    seafloor_slots,
    arrival_cells,
    ocean_state,
    ocean_kernels,
    shallow_mats,
    edge_proj,
    edge_lift,
    ocean_send,
    ocean_neighbours,
):
    anywhere = pl.BlockSpec(memory_space=pl.ANY)
    dma = pltpu.SemaphoreType.DMA
    I32 = jnp.int32
    inputs = (
        elastic,
        jacobian,
        jnp.transpose(star_mats, (1, 0, 2)),
        stiffness,
        jnp.transpose(face_proj, (1, 0, 2)),
        jnp.transpose(face_lift, (2, 0, 1)),
        clusters.reshape(1, E),
        lane_blocks(neighbours).reshape(-1),
        lane_blocks(send_faces).reshape(-1),
        fault_faces.reshape(1, 128),
        fault_strength.reshape(1, 128),
        seafloor_faces,
        seafloor_slots.reshape(1, 512),
        arrival_cells.reshape(8, 128),
        ocean_state,
        jnp.transpose(ocean_kernels, (1, 0, 2)),
        jnp.transpose(shallow_mats, (1, 0, 2)),
        jnp.transpose(edge_proj, (1, 0, 2)),
        jnp.transpose(edge_lift, (2, 0, 1)),
        ocean_send,
        lane_blocks(ocean_neighbours),
        fault_faces,
    )
    results = pl.pallas_call(
        main_kernel,
        out_shape=(
            jax.ShapeDtypeStruct(elastic.shape, BF16),
            jax.ShapeDtypeStruct(ocean_state.shape, F32),
        ),
        in_specs=[anywhere] * len(inputs),
        out_specs=(anywhere, anywhere),
        scratch_shapes=[
            pltpu.VMEM((NV, NB, E), BF16),
            pltpu.VMEM((3, E), F32),
            pltpu.VMEM((NV, 3, NV), F32),
            pltpu.VMEM((3, NB, NB), BF16),
            pltpu.VMEM((NF, 4, NB), BF16),
            pltpu.VMEM((NF, 4, NB), BF16),
            pltpu.VMEM((1, E), I32),
            pltpu.SMEM((4 * E,), I32),
            pltpu.SMEM((2 * BF,), I32),
            pltpu.VMEM((1, 128), I32),
            pltpu.SMEM((128,), I32),
            pltpu.VMEM((1, 128), F32),
            pltpu.SMEM((512,), I32),
            pltpu.VMEM((1, 512), I32),
            pltpu.VMEM((8, 128), I32),
            pltpu.VMEM((NO, NF, OC), F32),
            pltpu.VMEM((NF, 2, NF), F32),
            pltpu.VMEM((NO, 2, NO), F32),
            pltpu.VMEM((NE, 3, NF), F32),
            pltpu.VMEM((NE, 3, NF), F32),
            pltpu.SMEM((2, OBF), I32),
            pltpu.SMEM((OC // 128, 3, 128), I32),
            dma((22,)),
            pltpu.VMEM((1, E), F32),
            pltpu.VMEM((ROWS, E), F32),
            pltpu.VMEM((4 * ROWS, E), BF16),
            pltpu.VMEM((ROWS, 4 * ROWS), BF16),
            pltpu.VMEM((ROWS, 8 * MAIN), BF16),
            pltpu.VMEM((6 * MAIN, WIDE), BF16),
            pltpu.VMEM((ROWS, E), F32),
            pltpu.VMEM((2 * REST, MAIN), F32),
            pltpu.VMEM((E, 6 * MAIN), BF16),
            pltpu.VMEM((128, MAIN), F32),
            pltpu.VMEM((128, MAIN), F32),
            pltpu.VMEM((2, BF + 64, MAIN), BF16),
            pltpu.VMEM((2, BF + 64, MAIN), BF16),
            pltpu.VMEM((NV, NB, E), BF16),
            pltpu.VMEM((NO, NF, OC), F32),
            pltpu.VMEM((48, OC), F32),
            pltpu.VMEM((3 * OC + 2 * OBF + 2 * LEAD, 128), F32),
            pltpu.VMEM((3 * OC, 128), F32),
            pltpu.VMEM((2, OBF, 128), F32),
            pltpu.VMEM((2, OBF, 128), F32),
            pltpu.VMEM((48, OC), F32),
            pltpu.VMEM((512, 128), F32),
            pltpu.VMEM((128, 128), F32),
            pltpu.VMEM((N_DOM, 2, 128), F32),
            pltpu.VMEM((N_DOM, 2, 128), F32),
            pltpu.VMEM((N_SUB, 16, OC), F32),
            dma((2,)),
            dma((2,)),
            dma((2,)),
            dma((2,)),
            dma,
            dma,
            dma((3,)),
            dma((3,)),
            dma((NV + 1,)),
        ],
        compiler_params=pltpu.CompilerParams(
            collective_id=0,
            has_side_effects=True,
            vmem_limit_bytes=60 * 1024 * 1024,
        ),
    )(*inputs)
    return pl.pallas_call(
        place_kernel,
        out_shape=(
            jax.ShapeDtypeStruct(elastic.shape, BF16),
            jax.ShapeDtypeStruct(ocean_state.shape, F32),
        ),
        in_specs=[anywhere] * 2,
        out_specs=(anywhere, anywhere),
        scratch_shapes=[
            pltpu.VMEM((NV, NB, E), BF16),
            pltpu.VMEM((NO, NF, OC), F32),
            dma((NV + 1,)),
            dma((NV + 1,)),
        ],
        compiler_params=pltpu.CompilerParams(vmem_limit_bytes=60 * 1024 * 1024),
    )(*results)


def solution(mesh):
    both = ("dom", "sub")
    return jax.shard_map(
        body,
        mesh=mesh,
        in_specs=(
            P(None, None, both),
            P(None, both),
            P(),
            P(),
            P(),
            P(),
            P(both),
            P(None, both),
            P(None, both),
            P(both),
            P(both),
            P(both),
            P(both),
            P(both),
            P(None, None, "dom"),
            P(),
            P(),
            P(),
            P(),
            P(None, "dom"),
            P(None, "dom"),
        ),
        out_specs=(P(None, None, both), P(None, None, "dom")),
        check_vma=False,
    )
```
